128 devices in a mesh: queue: 16 (over y_hi, z, core), head: 8 (over y_lo, x).
Axes of the slice: x: 4, y: 4 (y_hi: 2, y_lo: 2; y = y_hi * 2 + y_lo), z: 4, core: 2. Of those that a mesh axis runs over, the one named last changes fastest.
Arguments:
- latent: bfloat16 [4096, 5120], P(('queue', 'head')), may hold values from -6 to 6
- fresh: bfloat16 [256, 5120], P('head'), may hold values from -6 to 6
- levels: int32 [16], replicated, may hold values from 0 to 47, as said below
- windows: int32 [16], replicated, may hold values from 1 to 16, as said below
- plan: int32 [48], replicated, may hold values from 20 to 975, as said below
- mod_table: float32 [3, 5120], replicated, may hold values from -3 to 3
- w_query: bfloat16 [5120, 4096], P(None, 'head'), may hold values from -0.078125 to 0.078125
- w_key: bfloat16 [5120, 4096], P(None, 'head'), may hold values from -0.078125 to 0.078125
- w_value: bfloat16 [5120, 4096], P(None, 'head'), may hold values from -0.078125 to 0.078125
- w_out: bfloat16 [4096, 5120], P('head'), may hold values from -0.09375 to 0.09375
- query_gain: float32 [4096], P('head'), may hold values from 0.7 to 4, as said below
- key_gain: float32 [4096], P('head'), may hold values from 0.7 to 4, as said below
Outputs:
- velocity: bfloat16 [2, 4096, 5120], P(None, ('queue', 'head'))
- updated: bfloat16 [4096, 5120], P(('queue', 'head'))
The draws below stay inside these ranges and needn't reach their ends.
Inputs may be any that keep to these rules, and one draw needn't show every extreme that they name: `levels`: strictly rising from slot to slot; the first slot has level 0 and the last level 47. `windows`: some slot has window 16 and some slot window 1. `plan`: strictly rising. `query_gain`: positive. `key_gain`: positive.
All inputs are finite; a program needn't handle non-finite values.
Results may differ from the reference program's by a relative error of at most 0.035.
Values may be sent and summed in bfloat16 or wider, within the bound.
No kernel may reach another device: no remote copies, remote signals or barrier semaphores. Data moves between devices by JAX's collectives and lax.ppermute only.
A program may use at most 128 MiB of HBM per device.

```python
import math
import jax
import jax.numpy as jnp
from jax import lax

D = 5120
HEADS = 32
HD = 128
LEVELS = 48
STEPS = 2
SLOTS = 16
SPAN = 256
TOKENS = 4096
N_HEAD = 8


def draw_levels(key, part):
    key = jax.random.fold_in(key, 11)
    inner = jax.random.permutation(key, LEVELS - 2)[:SLOTS - 2] + 1
    whole = jnp.concatenate([jnp.zeros((1,), jnp.int32), inner.astype(jnp.int32), jnp.full((1,), LEVELS - 1, jnp.int32)])
    return jnp.sort(whole).astype(jnp.int32)


def draw_windows(key, part):
    key = jax.random.fold_in(key, 12)
    first_key, second_key, third_key = jax.random.split(key, 3)
    base = jax.random.randint(first_key, (SLOTS,), 1, SLOTS + 1)
    widest = jax.random.randint(second_key, (), 0, SLOTS)
    narrow = (widest + 1 + jax.random.randint(third_key, (), 0, SLOTS - 1)) % SLOTS
    base = base.at[widest].set(SLOTS).at[narrow].set(1)
    return base.astype(jnp.int32)


def draw_plan(key, part):
    key = jax.random.fold_in(key, 13)
    jitter = jax.random.randint(key, (LEVELS,), 0, 16)
    jitter = jitter.at[0].set(0).at[LEVELS - 1].set(15)
    return (20 * (jnp.arange(LEVELS) + 1) + jitter).astype(jnp.int32)


def gain_values(key, lower, upper):
    return jnp.exp(jax.random.uniform(key, (HEADS * HD,), jnp.float32, math.log(lower), math.log(upper)))


def draw_query_gain(key, part):
    key = jax.random.fold_in(key, 14)
    return gain_values(key, 0.7, 4.0)


def draw_key_gain(key, part):
    key = jax.random.fold_in(key, 15)
    return gain_values(key, 0.7, 4.0)


def shard_levels(key, shape, shards, smallest, high):
    gain, own = 1.0, jax.random.fold_in(key, 6)
    for axis_at, blocks in shards:
        steps = jnp.exp(jax.random.uniform(jax.random.fold_in(own, axis_at), (blocks,), jnp.float32, smallest / len(shards), high / len(shards)))
        gain = gain * jnp.repeat(steps, shape[axis_at] // blocks).reshape([-1 if axis == axis_at else 1 for axis in range(len(shape))])
    return gain


def centred(rng, shape, scale, bound, cuts=(), held_as=jnp.bfloat16):
    entries = scale * jax.random.normal(rng, shape, jnp.float32)
    if cuts:
        entries = entries * shard_levels(rng, shape, cuts, -0.22, 0.18)
    return jnp.clip(entries, -bound, bound).astype(held_as)


def setup_inputs(seed: int = 0) -> dict:
    streams_of = jax.random.split(jax.random.key(seed), 13)
    latent = centred(streams_of[0], (TOKENS, D), 1.0, 6.0, ((0, 128),))
    fresh = centred(streams_of[1], (SPAN, D), 1.0, 6.0, ((0, 8),))
    levels = draw_levels(jax.random.fold_in(streams_of[12], 71), 0)
    windows = draw_windows(jax.random.fold_in(streams_of[12], 71), 0)
    plan = draw_plan(jax.random.fold_in(streams_of[12], 71), 0)
    mod_table = centred(streams_of[5], (3, D), 0.5, 3.0, (), jnp.float32)
    w_query = centred(streams_of[6], (D, HEADS * HD), D ** -0.5, 0.078125, ((1, 8),))
    w_key = centred(streams_of[7], (D, HEADS * HD), D ** -0.5, 0.078125, ((1, 8),))
    w_value = centred(streams_of[8], (D, HEADS * HD), D ** -0.5, 0.078125, ((1, 8),))
    w_out = centred(streams_of[9], (HEADS * HD, D), (HEADS * HD) ** -0.5, 0.09375, ((0, 8),))
    query_gain = draw_query_gain(jax.random.fold_in(streams_of[12], 71), 0)
    key_gain = draw_key_gain(jax.random.fold_in(streams_of[12], 71), 0)
    return dict(latent=latent, fresh=fresh, levels=levels, windows=windows, plan=plan, mod_table=mod_table, w_query=w_query, w_key=w_key, w_value=w_value, w_out=w_out, query_gain=query_gain, key_gain=key_gain)


def embed(times, width):
    half = width // 2
    freq = jnp.exp(-math.log(10000.0) * jnp.arange(half, dtype=jnp.float32) / half)
    angle = times[:, None] * freq[None, :]
    return jnp.concatenate([jnp.cos(angle), jnp.sin(angle)], axis=-1)

def forward(state, levels, windows, plan, mod_table, w_query, w_key, w_value, w_out, query_gain, key_gain, t_from):
    emb = embed(t_from, D)
    shift = mod_table[0][None, :] + emb
    scale = mod_table[1][None, :] + emb
    gate = mod_table[2][None, :] + emb
    x = state.astype(jnp.float32).reshape(SLOTS, SPAN, D)
    mean = lax.optimization_barrier(jnp.mean(x, axis=-1, keepdims=True))
    var = lax.optimization_barrier(jnp.mean((x - mean) ** 2, axis=-1, keepdims=True))
    h = ((x - mean) * lax.rsqrt(var + 1e-06) * (1.0 + scale[:, None, :]) + shift[:, None, :]).astype(jnp.bfloat16)
    flat = h.reshape(TOKENS, D)
    q = jnp.dot(flat, w_query, preferred_element_type=jnp.float32)
    k = jnp.dot(flat, w_key, preferred_element_type=jnp.float32)
    v = jnp.dot(flat, w_value, preferred_element_type=jnp.float32).astype(jnp.bfloat16)
    qn = (q * lax.rsqrt(lax.optimization_barrier(jnp.mean(q * q, axis=-1, keepdims=True)) + 1e-06) * query_gain).astype(jnp.bfloat16)
    kn = (k * lax.rsqrt(lax.optimization_barrier(jnp.mean(k * k, axis=-1, keepdims=True)) + 1e-06) * key_gain).astype(jnp.bfloat16)
    keys_all = kn.reshape(TOKENS, HEADS, HD).astype(jnp.float32)
    vals_all = v.reshape(TOKENS, HEADS, HD).astype(jnp.float32)
    span_ids = jnp.arange(TOKENS, dtype=jnp.int32) // SPAN

    def attend(index):
        lower = jnp.maximum(0, index - windows[index] + 1)
        valid = (span_ids >= lower) & (span_ids <= index)
        queries = lax.dynamic_slice_in_dim(qn, (index * SPAN).astype(jnp.int32), SPAN, 0)
        queries = queries.reshape(SPAN, HEADS, HD).astype(jnp.float32)
        scores = jnp.einsum('qhd,khd->hqk', queries, keys_all) / math.sqrt(HD)
        masked = jnp.where(valid[None, None, :], scores, -1e+30)
        top = lax.optimization_barrier(jnp.max(masked, axis=-1, keepdims=True))
        weights = jnp.where(valid[None, None, :], jnp.exp(scores - top), 0.0)
        total = lax.optimization_barrier(jnp.sum(weights, axis=-1))
        summed = jnp.einsum('hqk,khd->hqd', weights.astype(jnp.bfloat16).astype(jnp.float32), vals_all)
        out = summed / total[:, :, None]
        return jnp.transpose(out, (1, 0, 2)).reshape(SPAN, HEADS * HD).astype(jnp.bfloat16)
    attn = lax.map(attend, jnp.arange(SLOTS, dtype=jnp.int32)).reshape(TOKENS, HEADS * HD)
    group = HEADS * HD // N_HEAD
    o = jnp.zeros((TOKENS, D), jnp.float32)
    for index in range(N_HEAD):
        part = jnp.dot(attn[:, index * group:(index + 1) * group], w_out[index * group:(index + 1) * group], preferred_element_type=jnp.float32)
        o = o + part.astype(jnp.bfloat16).astype(jnp.float32)
    o = o.reshape(SLOTS, SPAN, D)
    return (x + gate[:, None, :] * o).astype(jnp.bfloat16).reshape(TOKENS, D)

def reference(latent, fresh, levels, windows, plan, mod_table, w_query, w_key, w_value, w_out, query_gain, key_gain):
    t_from = plan[levels].astype(jnp.float32)
    t_to = jnp.concatenate([jnp.zeros((1,), jnp.float32), t_from[:-1]])
    step_size = jnp.repeat((t_to - t_from) / 1000.0, SPAN)[:, None]
    state = latent
    speeds = []
    new = latent
    for step in range(STEPS):
        speed = forward(state, levels, windows, plan, mod_table, w_query, w_key, w_value, w_out, query_gain, key_gain, t_from)
        speeds.append(speed)
        new = (state.astype(jnp.float32) + step_size * speed.astype(jnp.float32)).astype(jnp.bfloat16)
        if step < STEPS - 1:
            state = jnp.concatenate([new[SPAN:], fresh], axis=0)
    return (jnp.stack(speeds), new)
```

```python
import functools
import math

import jax
import jax.numpy as jnp
from jax import lax
from jax.experimental import pallas as pl
from jax.experimental.pallas import tpu as pltpu
from jax.sharding import PartitionSpec as P

HD = 128
STEPS = 2
EXTRA = 16
F32, BF16 = jnp.float32, jnp.bfloat16
MIB = 1 << 20


def along_head(array, dx, dy):
    pairs = [(y * 4 + x, ((y + dy) % 2) * 4 + (x + dx) % 4) for y in range(2) for x in range(4)]
    return lax.ppermute(array, "head", pairs)


def along_queue(array, ds, dz, dc):
    pairs = [
        (s * 8 + z * 2 + c, ((s + ds) % 2) * 8 + ((z + dz) % 4) * 2 + (c + dc) % 2)
        for s in range(2)
        for z in range(4)
        for c in range(2)
    ]
    return lax.ppermute(array, "queue", pairs)


def embed(times, width):
    half = width // 2
    freq = jnp.exp(-math.log(10000.0) * jnp.arange(half, dtype=F32) / half)
    angle = times[:, None] * freq[None, :]
    return jnp.concatenate([jnp.cos(angle), jnp.sin(angle)], axis=-1)


def dot(a, b, lhs=1, rhs=0):
    return lax.dot_general(a, b, (((lhs,), (rhs,)), ((), ())), preferred_element_type=F32)


def row_sums(squares):
    ones = jnp.ones((8, squares.shape[1]), BF16)
    high = squares.astype(BF16)
    low = (squares - high.astype(F32)).astype(BF16)
    return dot(ones, high, 1, 1) + dot(ones, low, 1, 1)


def project_kernel(place, *refs):
    blocks, (wq, wk, wv, gq, gk), outs, acc = refs[:8], refs[8:13], refs[13:17], refs[17]
    keep_k, send_k, keep_qv, send_qv = outs
    step, side, core = pl.program_id(0), place[0], place[1]
    rows = jnp.concatenate([block[...] for block in blocks], axis=0)
    n = wq.shape[1]
    parts = [dot(rows, w[...]) for w in (wq, wk, wv)]

    @pl.when(step == 0)
    def _():
        for i, part in enumerate(parts):
            acc[:, i * n : (i + 1) * n] = part

    @pl.when(step > 0)
    def _():
        for i, part in enumerate(parts):
            acc[:, i * n : (i + 1) * n] += part

    @pl.when(step == pl.num_programs(0) - 1)
    def _():
        q, k, v = (acc[:, i * n : (i + 1) * n] for i in range(3))
        count = q.shape[0]
        sums_q, sums_k = row_sums(q * q), row_sums(k * k)
        lines = []
        for sums in (sums_q, sums_k):
            high = sums.astype(BF16).astype(F32)
            for part in (high, sums - high):
                lines += [part[:, :HD], part[:, HD:]]
        line = lax.broadcasted_iota(jnp.int32, (EXTRA, HD), 0)
        extra = jnp.zeros((EXTRA, HD), F32)
        for i, values in enumerate(lines):
            extra = jnp.where(line == i, jnp.concatenate([values, values], axis=0), extra)
        extra = extra.astype(BF16)
        q = (q * gq[...]).astype(BF16)
        k = (k * gk[...]).astype(BF16)
        v = v.astype(BF16)
        for head in range(4):
            own = jnp.where(side == head // 2, 0, 1)
            cut = slice(head * HD, (head + 1) * HD)

            def put(to_k, to_qv):
                to_k[own, :count] = k[:, cut]
                to_k[own, count:] = extra
                to_qv[own, 0] = q[:, cut]
                to_qv[own, 1] = v[:, cut]

            @pl.when(core == head % 2)
            def _():
                put(keep_k, keep_qv)

            @pl.when(core != head % 2)
            def _():
                put(send_k, send_qv)


def project(place, blocks, wq, wk, wv, gq, gk):
    block_rows, depth = blocks[0].shape
    rows, n, tile = 8 * block_rows, wq.shape[1], 1024
    k_shape = jax.ShapeDtypeStruct((2, rows + EXTRA, HD), BF16)
    qv_shape = jax.ShapeDtypeStruct((2, 2, rows, HD), BF16)
    whole = lambda shape: pl.BlockSpec(shape, lambda i, place: (0,) * len(shape))
    return pl.pallas_call(
        project_kernel,
        grid_spec=pltpu.PrefetchScalarGridSpec(
            num_scalar_prefetch=1,
            grid=(depth // tile,),
            in_specs=[pl.BlockSpec((block_rows, tile), lambda i, place: (0, i))] * 8
            + [pl.BlockSpec((tile, n), lambda i, place: (i, 0))] * 3
            + [whole((1, n))] * 2,
            out_specs=[whole(k_shape.shape)] * 2 + [whole(qv_shape.shape)] * 2,
            scratch_shapes=[pltpu.VMEM((rows, 3 * n), F32)],
        ),
        out_shape=[k_shape, k_shape, qv_shape, qv_shape],
        compiler_params=pltpu.CompilerParams(vmem_limit_bytes=40 * MIB),
        cost_estimate=pl.CostEstimate(
            flops=6 * rows * depth * n, bytes_accessed=6 * depth * n, transcendentals=0
        ),
        name="project",
    )(place, *blocks, wq, wk, wv, gq[None, :], gk[None, :])


def attend_kernel(every, slots, lowers, places, sums, q, *refs):
    ks, vs, (o_own, o_sib, o_far), (keys, values, totals) = refs[:4], refs[4:8], refs[8:11], refs[11:]
    count = q.shape[2]
    scale = lax.rsqrt(sums[...] * (1.0 / every) + 1e-6)
    pad = jnp.zeros((HD - 16, HD), F32)
    lines = [
        jnp.concatenate([scale[:, i * HD : (i + 1) * HD], pad], axis=0).T for i in range(4)
    ]
    q_scale = jnp.concatenate(lines[:2], axis=0)
    k_scale = jnp.concatenate(lines[2:], axis=0)
    for at in range(16):
        where = places[at]
        k = ks[at // 4][at % 4, :count].astype(F32)
        keys[where] = (k * k_scale[:, at : at + 1]).astype(BF16)
        values[where] = vs[at // 4][at % 4]
    for span, out in enumerate((o_own.at[:], o_sib.at[:], o_far.at[0], o_far.at[1])):
        queries = q[span // 2, span % 2].astype(F32) * (
            q_scale[:, span : span + 1] * (1.0 / math.sqrt(HD))
        )
        queries = queries.astype(BF16)

        def block(j, carry):
            top, total, acc = carry
            scores = dot(keys[j], queries, 1, 1)
            new_top = jnp.maximum(top, jnp.max(scores, axis=0, keepdims=True))
            weights = jnp.exp(scores - new_top)
            fade = jnp.exp(top - new_top)
            total = total * fade + jnp.sum(weights, axis=0, keepdims=True)
            acc = acc * fade + dot(values[j], weights.astype(BF16), 0, 0)
            return new_top, total, acc

        start = (
            jnp.full((1, count), -1e30, F32),
            jnp.zeros((1, count), F32),
            jnp.zeros((HD, count), F32),
        )
        _, total, acc = lax.fori_loop(lowers[span], slots[span] + 1, block, start)
        out[...] = (acc / total).T.astype(BF16)


def attend(slots, lowers, places, sums, q, ks, vs, every):
    rows = q.shape[2]
    out = jax.ShapeDtypeStruct((rows, HD), BF16)
    vmem = pl.BlockSpec(memory_space=pltpu.VMEM)
    smem = pl.BlockSpec(memory_space=pltpu.SMEM)
    return pl.pallas_call(
        functools.partial(attend_kernel, every),
        in_specs=[smem] * 3 + [vmem] * 10,
        out_specs=[vmem] * 3,
        out_shape=[out, out, jax.ShapeDtypeStruct((2, rows, HD), BF16)],
        scratch_shapes=[
            pltpu.VMEM((16, rows, HD), BF16),
            pltpu.VMEM((16, rows, HD), BF16),
            pltpu.VMEM((8, rows), F32),
        ],
        compiler_params=pltpu.CompilerParams(vmem_limit_bytes=40 * MIB),
        cost_estimate=pl.CostEstimate(
            flops=4 * 32 * rows * rows * HD, bytes_accessed=4 * MIB, transcendentals=32 * rows * rows
        ),
        name="attend",
    )(slots, lowers, places, sums, q, *ks, *vs)


def mix_kernel(place, own, far, near, w, out, acts):
    side, core = place[0], place[1]
    rows = own.shape[0]

    @pl.when(pl.program_id(0) == 0)
    def _():
        for values, s, c in (
            (own[...], side, core),
            (far[0], 1 - side, core),
            (near[0], side, 1 - core),
            (near[1], 1 - side, 1 - core),
        ):
            acts[:, pl.ds(pl.multiple_of((2 * s + c) * HD, HD), HD)] = values

    product = dot(acts[...], w[...]).astype(BF16)
    step = rows // 8
    for i in range(8):
        out[place[2 + i]] = product[i * step : (i + 1) * step]


def mix(place, own, far, near, w):
    rows, depth, width, tile = own.shape[0], w.shape[0], w.shape[1], 1024
    whole = lambda shape: pl.BlockSpec(shape, lambda i, place: (0,) * len(shape))
    return pl.pallas_call(
        mix_kernel,
        grid_spec=pltpu.PrefetchScalarGridSpec(
            num_scalar_prefetch=1,
            grid=(width // tile,),
            in_specs=[whole(own.shape), whole(far.shape), whole(near.shape)]
            + [pl.BlockSpec((depth, tile), lambda i, place: (0, i))],
            out_specs=pl.BlockSpec((8, rows // 8, tile), lambda i, place: (0, 0, i)),
            scratch_shapes=[pltpu.VMEM((rows, depth), BF16)],
        ),
        out_shape=jax.ShapeDtypeStruct((8, rows // 8, width), BF16),
        compiler_params=pltpu.CompilerParams(vmem_limit_bytes=40 * MIB),
        cost_estimate=pl.CostEstimate(
            flops=2 * rows * depth * width, bytes_accessed=2 * depth * width, transcendentals=0
        ),
        name="mix",
    )(place, own, far, near, w)


def gather_blocks(block):
    left, right = along_head(block, 1, 0), along_head(block, -1, 0)
    other = along_head(block, 0, 1)
    across = along_head(block, 2, 0)
    other_left, other_right = along_head(other, 1, 0), along_head(other, -1, 0)
    other_across = along_head(across, 0, 1)
    return [block, right, across, left, other, other_right, other_across, other_left]


def sum_over_head(sums):
    turn = lambda array, by: jnp.concatenate([array[:, :, :, by:], array[:, :, :, :by]], axis=3)
    sums = sums + turn(along_head(sums, 1, 0), 1)
    sums = sums + turn(along_head(sums, 2, 0), 2)
    return sums + along_head(sums, 0, 1)[:, :, ::-1]


def on_device(
    latent, fresh, levels, windows, plan, mod_table, w_query, w_key, w_value, w_out, query_gain, key_gain
):
    queue_count, head_count = lax.axis_size("queue"), lax.axis_size("head")
    slot, head = lax.axis_index("queue"), lax.axis_index("head")
    rows = latent.shape[0]
    span = rows * head_count
    every = w_query.shape[1] * head_count
    side, z, core = slot // 8, (slot // 2) % 4, slot % 2
    places = jnp.stack(
        [
            ((side + s) % 2) * 8 + ((z + dz) % 4) * 2 + (core + c) % 2
            for dz in range(4)
            for s in range(2)
            for c in range(2)
        ]
    )
    blocks_at = [((head // 4 + dy) % 2) * 4 + (head % 4 + dx) % 4 for dy in range(2) for dx in range(4)]
    place = jnp.stack([side, core] + blocks_at)
    lower_all = jnp.maximum(0, jnp.arange(queue_count, dtype=jnp.int32) - windows + 1)
    q_slots = places[:4]
    q_lowers = lower_all[q_slots]

    table_hits = levels[:, None] == jnp.arange(plan.shape[0], dtype=jnp.int32)[None, :]
    t_all = jnp.sum(jnp.where(table_hits, plan[None, :], 0), axis=1).astype(F32)
    t_from = t_all[slot]
    t_to = jnp.where(slot > 0, t_all[jnp.maximum(slot - 1, 0)], 0.0)
    step_size = (t_to - t_from) / 1000.0
    emb = embed(t_from[None], latent.shape[1])[0]
    shift = mod_table[0] + emb
    scale = mod_table[1] + emb
    gate = mod_table[2] + emb
    state = latent
    speeds = []
    new = latent
    for step in range(STEPS):
        with jax.named_scope("norm"):
            x = state.astype(F32)
            mean = jnp.mean(x, axis=-1, keepdims=True)
            var = jnp.mean((x - mean) ** 2, axis=-1, keepdims=True)
            normed = ((x - mean) * lax.rsqrt(var + 1e-06) * (1.0 + scale) + shift).astype(BF16)
        with jax.named_scope("gather"):
            blocks = gather_blocks(normed)
        with jax.named_scope("project"):
            keep_k, send_k, keep_qv, send_qv = project(
                place, blocks, w_query, w_key, w_value, query_gain, key_gain
            )
        with jax.named_scope("swap"):
            core_k = along_queue(send_k, 0, 0, 1)
            core_qv = along_queue(send_qv, 0, 0, 1)
            far_k = along_queue(jnp.stack([keep_k[1], core_k[1]]), 1, 0, 0)
            own_k = jnp.stack([keep_k[0], core_k[0], far_k[0], far_k[1]])
            far_qv = along_queue(jnp.stack([keep_qv[1], core_qv[1]]), 1, 0, 0)
            own_v = jnp.stack([keep_qv[0, 1], core_qv[0, 1], far_qv[0, 1], far_qv[1, 1]])
            own_q = jnp.stack([keep_qv[0, 0], core_qv[0, 0], far_qv[0, 0], far_qv[1, 0]]).reshape(
                2, 2, span, HD
            )
        with jax.named_scope("ring"):
            ks = [own_k] + [along_queue(own_k, 0, -dz, 0) for dz in (1, 2, 3)]
            vs = [own_v] + [along_queue(own_v, 0, -dz, 0) for dz in (1, 2, 3)]
        with jax.named_scope("sums"):
            lines = jnp.concatenate([k[:, span : span + 8] for k in ks], axis=0).astype(F32)
            lines = lines.reshape(16, 2, 2, 2, HD)
            sums = (lines[:, :, 0] + lines[:, :, 1]).reshape(16, 2, 2, 4, HD // 4)
            sums = sum_over_head(sums).reshape(16, 4 * HD)
        with jax.named_scope("attend"):
            o_own, o_sib, o_far = attend(q_slots, q_lowers, places, sums, own_q, ks, vs, every)
        with jax.named_scope("back"):
            far = along_queue(o_far, 1, 0, 0)
            near = along_queue(jnp.stack([o_sib, far[1]]), 0, 0, 1)
        with jax.named_scope("mix"):
            product = mix(place, o_own, far, near, w_out)
        with jax.named_scope("reduce"):
            mixed = jnp.sum(lax.all_to_all(product, "head", 0, 0).astype(F32), axis=0)
        with jax.named_scope("update"):
            speed = (x + gate * mixed).astype(BF16)
            speeds.append(speed)
            new = (x + step_size * speed.astype(F32)).astype(BF16)
            if step < STEPS - 1:
                moved = lax.ppermute(new, "queue", [(i, i - 1) for i in range(1, queue_count)])
                state = jnp.where(slot == queue_count - 1, fresh, moved)
    return (jnp.stack(speeds), new)


def solution(mesh):
    return jax.shard_map(
        on_device,
        mesh=mesh,
        in_specs=(
            P(("queue", "head"), None),
            P("head", None),
            P(),
            P(),
            P(),
            P(),
            P(None, "head"),
            P(None, "head"),
            P(None, "head"),
            P("head", None),
            P("head"),
            P("head"),
        ),
        out_specs=(P(None, ("queue", "head"), None), P(("queue", "head"), None)),
        check_vma=False,
    )
```

```python
import functools
import math

import jax
import jax.numpy as jnp
from jax import lax
from jax.experimental import pallas as pl
from jax.experimental.pallas import tpu as pltpu
from jax.sharding import PartitionSpec as P

HD = 128
STEPS = 2
EXTRA = 16
F32, BF16 = jnp.float32, jnp.bfloat16
MIB = 1 << 20
VMEM_LIMIT = 8 * MIB
ALL_VMEM = 60 * MIB
LOAD_VMEM = 36 * MIB
MIX_VMEM = 48 * MIB
MIX_PARTS = 4


def along_head(array, dx, dy):
    pairs = [(y * 4 + x, ((y + dy) % 2) * 4 + (x + dx) % 4) for y in range(2) for x in range(4)]
    return lax.ppermute(array, "head", pairs)


def along_queue(array, ds, dz, dc):
    pairs = [
        (s * 8 + z * 2 + c, ((s + ds) % 2) * 8 + ((z + dz) % 4) * 2 + (c + dc) % 2)
        for s in range(2)
        for z in range(4)
        for c in range(2)
    ]
    return lax.ppermute(array, "queue", pairs)


def dot(a, b, lhs=1, rhs=0):
    return lax.dot_general(a, b, (((lhs,), (rhs,)), ((), ())), preferred_element_type=F32)


def load_kernel(*refs):
    count = len(refs) // 2
    sources, outs, arrived = refs[:count], refs[count : 2 * count], refs[-1]
    copies = [pltpu.make_async_copy(a, b, arrived.at[i]) for i, (a, b) in enumerate(zip(sources, outs))]
    for copy in copies:
        copy.start()
    for copy in copies:
        copy.wait()


def load(arrays):
    return pl.pallas_call(
        load_kernel,
        in_specs=[pl.BlockSpec(memory_space=pl.ANY)] * len(arrays),
        out_specs=[pl.BlockSpec(memory_space=pltpu.VMEM)] * len(arrays),
        out_shape=[jax.ShapeDtypeStruct(array.shape, array.dtype) for array in arrays],
        scratch_shapes=[pltpu.SemaphoreType.DMA((len(arrays),))],
        compiler_params=pltpu.CompilerParams(vmem_limit_bytes=LOAD_VMEM),
        cost_estimate=pl.CostEstimate(
            flops=0, bytes_accessed=sum(2 * array.size for array in arrays), transcendentals=0
        ),
        name="load",
    )(*arrays)


def project_kernel(place, *refs):
    blocks, weights, gains, (keep, send, rows, extra) = refs[:8], refs[8:11], refs[11], refs[12:]
    side, core = place[0], place[1]
    step, count = blocks[0].shape[0], rows.shape[0]
    for i, block in enumerate(blocks):
        rows[i * step : (i + 1) * step] = block[...]
    squares = {}
    for kind, w in enumerate(weights):
        part = dot(rows[...], w[...])
        if kind != 1:
            tiles = [part[:, i : i + HD] for i in range(0, part.shape[1], HD)]
            squares[kind] = sum(tile * tile for tile in tiles)
            part = part * gains[kind // 2 : kind // 2 + 1]
        part = part.astype(BF16)
        for pair in range(2):
            first, second = (part[:, (2 * pair + i) * HD : (2 * pair + i + 1) * HD] for i in range(2))
            at = jnp.where(side == pair, 0, 3) + kind
            to = pl.ds(pl.multiple_of(at * count, count), count)

            @pl.when(core == 0)
            def _():
                keep[to, :] = first
                send[to, :] = second

            @pl.when(core == 1)
            def _():
                keep[to, :] = second
                send[to, :] = first

    for i, kind in enumerate((2, 0)):
        for half in range(2):
            line = jnp.sum(squares[kind][half * HD : (half + 1) * HD].T, axis=0, keepdims=True)
            high = line.astype(BF16).astype(F32)
            at = i * 2 + half
            extra[at : at + 1] = high
            extra[8 + at : 9 + at] = line - high
    for at in (4, 12):
        extra[at : at + 4] = jnp.zeros((4, HD), F32)
    keep[6 * count :] = extra[...].astype(BF16)
    send[6 * count :] = extra[...].astype(BF16)


def project(place, blocks, wk, wv, wq, gains):
    block_rows, depth = blocks[0].shape
    rows, n = 8 * block_rows, wq.shape[1]
    out = jax.ShapeDtypeStruct((6 * rows + EXTRA, HD), BF16)
    vmem = pl.BlockSpec(memory_space=pltpu.VMEM)
    return pl.pallas_call(
        project_kernel,
        in_specs=[pl.BlockSpec(memory_space=pltpu.SMEM)] + [vmem] * 12,
        out_specs=[vmem] * 2,
        out_shape=[out, out],
        scratch_shapes=[pltpu.VMEM((rows, depth), BF16), pltpu.VMEM((EXTRA, HD), F32)],
        compiler_params=pltpu.CompilerParams(vmem_limit_bytes=VMEM_LIMIT),
        cost_estimate=pl.CostEstimate(
            flops=6 * rows * depth * n, bytes_accessed=6 * depth * n, transcendentals=0
        ),
        name="project",
    )(place, *blocks, wk, wv, wq, gains)


def assemble_kernel(keep, swapped, near, far, far_queries, sums):
    count = near.shape[0] // 4
    for i, ref in enumerate((keep, swapped)):
        near[2 * i * count : 2 * (i + 1) * count] = ref[: 2 * count]
        far[2 * i * count : 2 * (i + 1) * count] = ref[3 * count : 5 * count]
        far_queries[i * count : (i + 1) * count] = ref[5 * count : 6 * count]
        extra = ref[6 * count :].astype(F32)
        sums[4 * i : 4 * (i + 1)] = extra[:4] + extra[8:12]


def assemble(keep, swapped):
    vmem = pl.BlockSpec(memory_space=pltpu.VMEM)
    rows = (keep.shape[0] - EXTRA) // 6
    return pl.pallas_call(
        assemble_kernel,
        in_specs=[vmem] * 2,
        out_specs=[vmem] * 4,
        out_shape=[
            jax.ShapeDtypeStruct((4 * rows, HD), BF16),
            jax.ShapeDtypeStruct((4 * rows, HD), BF16),
            jax.ShapeDtypeStruct((2 * rows, HD), BF16),
            jax.ShapeDtypeStruct((8, HD), F32),
        ],
        compiler_params=pltpu.CompilerParams(vmem_limit_bytes=VMEM_LIMIT),
        name="assemble",
    )(keep, swapped)


def row_scales(lines, every):
    scales = lax.rsqrt(lines * (1.0 / every) + 1e-6)
    return jnp.concatenate([scales, jnp.zeros((HD - lines.shape[0], HD), F32)], axis=0).T


def scale_column(scales, span, kind):
    at = 4 * span + 2 * kind
    return jnp.concatenate([scales[:, at : at + 1], scales[:, at + 1 : at + 2]], axis=0)


def attend_span(queries, scale, lower, slot, keys, values):
    rows = queries.shape[0]
    queries = (queries.astype(F32) * scale).astype(BF16)

    def absorb(width):
        def block(j, carry):
            top, total, acc = carry
            part = pl.ds(pl.multiple_of(j * rows, rows), width * rows)
            scores = dot(keys[part, :], queries, 1, 1)
            new_top = jnp.maximum(top, jnp.max(scores, axis=0, keepdims=True))
            weights = jnp.exp2(scores - new_top)
            fade = jnp.exp2(top - new_top)
            total = total * fade + jnp.sum(weights, axis=0, keepdims=True)
            acc = acc * fade + dot(values[part, :], weights.astype(BF16), 0, 0)
            return new_top, total, acc

        return block

    carry = (
        jnp.full((1, rows), -1e30, F32),
        jnp.zeros((1, rows), F32),
        jnp.zeros((HD, rows), F32),
    )
    count = slot + 1 - lower
    at = lower
    for width in WIDTHS:
        times = count // width
        carry = lax.fori_loop(0, times, lambda i, c, w=width, a=at: absorb(w)(a + i * w, c), carry)
        at, count = at + times * width, count - times * width
    _, total, acc = carry
    return (acc / total).T.astype(BF16)


LOG2_SCALE = math.log2(math.e) / math.sqrt(HD)
WIDTHS = (8, 4, 2, 1)


def attend_far_kernel(every, place, *refs):
    pairs, (queries, near_sums, far_sums), (out, keys, values) = refs[:8], refs[8:11], refs[11:]
    rows = out.shape[1]
    near_scales = row_scales(near_sums[...], every)
    far_scales = row_scales(far_sums[...], every)
    for at in range(16):
        scales = far_scales if at % 4 // 2 else near_scales
        ref, first = pairs[at // 4 + 4 * (at % 4 // 2)], 2 * (at % 2) * rows
        to = pl.ds(pl.multiple_of(place[8 + at] * rows, rows), rows)
        scale = scale_column(scales, 2 * (at // 4) + at % 2, 1)
        keys[to, :] = (ref[first : first + rows].astype(F32) * scale).astype(BF16)
        values[to, :] = ref[first + rows : first + 2 * rows]
    for span in range(2):
        out[span] = attend_span(
            queries[span * rows : (span + 1) * rows],
            scale_column(far_scales, span, 0) * LOG2_SCALE,
            place[6 + span],
            place[2 + span],
            keys,
            values,
        )


def attend_near_kernel(every, place, sums, keep, swapped, keys, values, out_own, out_sib):
    rows = out_own.shape[0]
    scales = row_scales(sums[...], every)
    for span, (queries, out) in enumerate(((keep, out_own), (swapped, out_sib))):
        out[...] = attend_span(
            queries[2 * rows : 3 * rows],
            scale_column(scales, span, 0) * LOG2_SCALE,
            place[4 + span],
            place[span],
            keys,
            values,
        )


def attend_cost(rows):
    return pl.CostEstimate(flops=4 * 16 * rows * rows * HD, bytes_accessed=2 * MIB, transcendentals=16 * rows * rows)


def attend_far(place, pairs, queries, near_sums, far_sums, every):
    rows = pairs[0].shape[0] // 4
    vmem, smem = pl.BlockSpec(memory_space=pltpu.VMEM), pl.BlockSpec(memory_space=pltpu.SMEM)
    spans = jax.ShapeDtypeStruct((16 * rows, HD), BF16)
    return pl.pallas_call(
        functools.partial(attend_far_kernel, every),
        in_specs=[smem] + [vmem] * 11,
        out_specs=[vmem] * 3,
        out_shape=[jax.ShapeDtypeStruct((2, rows, HD), BF16), spans, spans],
        compiler_params=pltpu.CompilerParams(vmem_limit_bytes=VMEM_LIMIT),
        cost_estimate=attend_cost(rows),
        name="attend_far",
    )(place, *pairs, queries, near_sums, far_sums)


def attend_near(place, sums, keep, swapped, keys, values, every):
    rows = keys.shape[0] // 16
    vmem, smem = pl.BlockSpec(memory_space=pltpu.VMEM), pl.BlockSpec(memory_space=pltpu.SMEM)
    out = jax.ShapeDtypeStruct((rows, HD), BF16)
    return pl.pallas_call(
        functools.partial(attend_near_kernel, every),
        in_specs=[smem] + [vmem] * 5,
        out_specs=[vmem] * 2,
        out_shape=[out, out],
        compiler_params=pltpu.CompilerParams(vmem_limit_bytes=VMEM_LIMIT),
        cost_estimate=attend_cost(rows),
        name="attend_near",
    )(place, sums, keep, swapped, keys, values)


def mix_kernel(place, own, far, near, near_far, w, *refs):
    outs, (acts, held, arrived) = refs[:8], refs[8:]
    part = w.shape[0] // MIX_PARTS
    parts = [pl.ds(i * part, part) for i in range(MIX_PARTS)]
    copies = [pltpu.make_async_copy(w.at[at], held.at[at], arrived.at[i]) for i, at in enumerate(parts)]
    for copy in copies:
        copy.start()
    side, core = place[0], place[1]
    for values, s, c in (
        (own[...], side, core),
        (far[0], 1 - side, core),
        (near[...], side, 1 - core),
        (near_far[1], 1 - side, 1 - core),
    ):
        acts[:, pl.ds(pl.multiple_of((2 * s + c) * HD, HD), HD)] = values
    for copy in copies:
        copy.wait()
    step, width, tile = acts.shape[0] // 8, w.shape[1], 512
    for i in range(0, width, tile):
        product = dot(acts[...], held[:, i : i + tile]).astype(BF16)
        for at, out in enumerate(outs):
            out[:, i : i + tile] = product[at * step : (at + 1) * step]


def mix(place, own, far, near, near_far, w):
    rows, depth, width = own.shape[0], w.shape[0], w.shape[1]
    vmem = pl.BlockSpec(memory_space=pltpu.VMEM)
    return pl.pallas_call(
        mix_kernel,
        in_specs=[pl.BlockSpec(memory_space=pltpu.SMEM)] + [vmem] * 4 + [pl.BlockSpec(memory_space=pl.ANY)],
        out_specs=[vmem] * 8,
        out_shape=[jax.ShapeDtypeStruct((rows // 8, width), BF16)] * 8,
        scratch_shapes=[
            pltpu.VMEM((rows, depth), BF16),
            pltpu.VMEM(w.shape, BF16),
            pltpu.SemaphoreType.DMA((MIX_PARTS,)),
        ],
        compiler_params=pltpu.CompilerParams(vmem_limit_bytes=MIX_VMEM),
        cost_estimate=pl.CostEstimate(
            flops=2 * rows * depth * width, bytes_accessed=2 * depth * width, transcendentals=0
        ),
        name="mix",
    )(place, own, far, near, near_far, w)


def norm_rows(x, scale, shift):
    mean = jnp.mean(x, axis=-1, keepdims=True)
    var = jnp.mean((x - mean) ** 2, axis=-1, keepdims=True)
    return ((x - mean) * lax.rsqrt(var + 1e-06) * (1.0 + scale) + shift).astype(BF16)


def start_kernel(place, levels_at, plan_at, x_at, table_at, out, mods, levels, plan, x, table, arrived):
    pairs = ((levels_at, levels), (plan_at, plan), (table_at, table), (x_at, x))
    copies = [pltpu.make_async_copy(a, b, arrived.at[i]) for i, (a, b) in enumerate(pairs)]
    for copy in copies:
        copy.start()
    half = table.shape[1] // 2
    at = lax.broadcasted_iota(jnp.int32, (8, half), 1).astype(F32)
    freq = jnp.exp(-math.log(10000.0) * at / half)
    line = lax.broadcasted_iota(jnp.int32, (8, half), 0)
    for copy in copies:
        copy.wait()
    slot = place[2]
    t_from, t_below = (plan[levels[place[2 + i]]].astype(F32) for i in range(2))
    angle = jnp.where(line < 3, t_from, t_below) * freq
    emb = jnp.concatenate([jnp.cos(angle), jnp.sin(angle)], axis=1)
    values = table[...]
    mods[...] = jnp.concatenate([values, values[:2], values], axis=0) + emb
    mods[5:6] = jnp.full((1, 2 * half), (jnp.where(slot > 0, t_below, 0.0) - t_from) / 1000.0, F32)
    mods[6:7] = jnp.full((1, 2 * half), jnp.where(slot == 0, 1.0, 0.0), F32)
    out[...] = norm_rows(x[...].astype(F32), mods[1:2], mods[0:1])


def start(place, levels, plan, x, table):
    vmem, smem = pl.BlockSpec(memory_space=pltpu.VMEM), pl.BlockSpec(memory_space=pltpu.SMEM)
    hbm = pl.BlockSpec(memory_space=pl.ANY)
    return pl.pallas_call(
        start_kernel,
        in_specs=[smem] + [hbm] * 4,
        out_specs=[vmem] * 2,
        out_shape=[jax.ShapeDtypeStruct(x.shape, BF16), jax.ShapeDtypeStruct((8, x.shape[1]), F32)],
        scratch_shapes=[
            pltpu.SMEM(levels.shape, jnp.int32),
            pltpu.SMEM(plan.shape, jnp.int32),
            pltpu.VMEM(x.shape, BF16),
            pltpu.VMEM(table.shape, F32),
            pltpu.SemaphoreType.DMA((4,)),
        ],
        compiler_params=pltpu.CompilerParams(vmem_limit_bytes=ALL_VMEM),
        name="start",
    )(place, levels, plan, x, table)


def stepped(x, mods, parts):
    mixed = parts[0][...].astype(F32)
    for part in parts[1:]:
        mixed += part[...].astype(F32)
    x = x[...].astype(F32)
    speed = (x + mods[2:3] * mixed).astype(BF16)
    return speed, (x + mods[5:6] * speed.astype(F32)).astype(BF16)


def middle_kernel(x, mods, fresh, *refs):
    parts, (speed_out, state_out, normed_out) = refs[:-3], refs[-3:]
    speed, new = stepped(x, mods, parts)
    speed_out[...] = speed
    state = jnp.where(mods[6:7] > 0.5, fresh[...].astype(F32), new.astype(F32))
    state_out[...] = state.astype(BF16)
    normed_out[...] = norm_rows(state, mods[4:5], mods[3:4])


def last_kernel(x, mods, before, *refs):
    parts, (speeds_out, new_out) = refs[:-2], refs[-2:]
    speed, new = stepped(x, mods, parts)
    speeds_out[0] = before[...]
    speeds_out[1] = speed
    new_out[...] = new


def update(kernel, name, x, mods, other, parts, shapes):
    vmem = pl.BlockSpec(memory_space=pltpu.VMEM)
    return pl.pallas_call(
        kernel,
        in_specs=[vmem] * (3 + len(parts)),
        out_specs=[vmem] * len(shapes),
        out_shape=[jax.ShapeDtypeStruct(shape, BF16) for shape in shapes],
        compiler_params=pltpu.CompilerParams(vmem_limit_bytes=VMEM_LIMIT),
        name=name,
    )(x, mods, other, *parts)


def one_down(array, dx, dy):
    queue = lax.axis_size("queue")
    pairs = [
        (q * 8 + y * 4 + x, ((q - 1) % queue) * 8 + ((y + dy) % 2) * 4 + (x + dx) % 4)
        for q in range(queue)
        for y in range(2)
        for x in range(4)
    ]
    return lax.ppermute(array, ("queue", "head"), pairs)


def gather_blocks(block, move):
    other = move(block, 0, 1)
    left, right, across = move(block, 1, 0), move(block, -1, 0), move(block, 2, 0)
    other_left, other_right = along_head(other, 1, 0), along_head(other, -1, 0)
    other_across = along_head(across, 0, 1)
    return [right, across, left, other, other_right, other_across, other_left]


def scatter_blocks(blocks):
    own, right, across, left, other, other_right, other_across, other_left = blocks
    add = lambda *terms: sum(term.astype(F32) for term in terms).astype(BF16)
    from_left, from_right = along_head(other_right, 1, 0), along_head(other_left, -1, 0)
    from_other = along_head(other_across, 0, 1)
    gets = [along_head(right, 1, 0), along_head(left, -1, 0)]
    gets.append(along_head(add(other, from_left, from_right), 0, 1))
    gets.append(along_head(add(across, from_other), 2, 0))
    return [own] + gets


def turned(sums, by):
    by *= HD // 4
    return jnp.concatenate([sums[:, by:], sums[:, :by]], axis=1)


def on_device(
    latent, fresh, levels, windows, plan, mod_table, w_query, w_key, w_value, w_out, query_gain, key_gain
):
    queue_count, head_count = lax.axis_size("queue"), lax.axis_size("head")
    slot = lax.axis_index("queue")
    rows = latent.shape[0]
    span = rows * head_count
    every = w_query.shape[1] * head_count
    side, z, core = slot // 8, (slot // 2) % 4, slot % 2
    place = jnp.stack([side, core, slot, (slot + queue_count - 1) % queue_count])
    places = jnp.stack(
        [
            ((side + s) % 2) * 8 + ((z + dz) % 4) * 2 + (core + c) % 2
            for dz in range(4)
            for s in range(2)
            for c in range(2)
        ]
    )
    lowers = jnp.maximum(0, jnp.arange(queue_count, dtype=jnp.int32) - windows + 1)
    order = jnp.concatenate([places[:4], lowers[places[:4]], places])

    gains = jnp.stack([key_gain, query_gain])

    x = latent
    normed, mods = start(place, levels, plan, x, mod_table)
    blocks = [normed] + gather_blocks(normed, along_head)
    weights = load([w_key, w_value, w_query])
    for step in range(STEPS):
        with jax.named_scope("project"):
            keep, send = project(place, blocks, *weights, gains)
        with jax.named_scope("swap"):
            swapped = along_queue(send, 0, 0, 1)
            near, far, queries, sums = assemble(keep, swapped)
        with jax.named_scope("round1"):
            near1, near3 = along_queue(near, 0, -1, 0), along_queue(near, 0, 1, 0)
            far = along_queue(far, 1, 0, 0)
            others = [along_head(sums, by, 0) for by in (1, 2, 3)]
            near1, near3, far, others = lax.optimization_barrier((near1, near3, far, others))
            for by in (1, 2, 3):
                sums += turned(others[by - 1], by)
            near, queries, sums = lax.optimization_barrier((near, queries, sums))
        with jax.named_scope("round2"):
            near2 = along_queue(near, 0, -2, 0)
            other = along_head(sums, 0, 1)
            queries = along_queue(queries, 1, 0, 0)
            near2, other, queries = lax.optimization_barrier((near2, other, queries))
            sums += other.reshape(4, 2, HD)[:, ::-1].reshape(8, HD)
            far, sums = lax.optimization_barrier((far, sums))
        with jax.named_scope("round3"):
            far1, far3 = along_queue(far, 0, -1, 0), along_queue(far, 0, 1, 0)
            near_sums = [sums] + [along_queue(sums, 0, -dz, 0) for dz in (1, 2, 3)]
            far1, far3, near_sums = lax.optimization_barrier((far1, far3, near_sums))
            near_sums, far = lax.optimization_barrier((jnp.concatenate(near_sums, axis=0), far))
        with jax.named_scope("round4"):
            far2 = along_queue(far, 0, -2, 0)
            far_sums = along_queue(near_sums, 1, 0, 0)
        with jax.named_scope("attend"):
            if step > 0:
                state, far_sums = lax.optimization_barrier((state, far_sums))
                x = one_down(state, 0, 0)
            pairs = [near, near1, near2, near3, far, far1, far2, far3]
            o_far, keys, values = attend_far(order, pairs, queries, near_sums, far_sums, every)
            far = along_queue(o_far, 1, 0, 0)
            o_own, o_sib = attend_near(order, sums, keep, swapped, keys, values, every)
            far, o_sib = lax.optimization_barrier((far, o_sib))
            o_near = along_queue(o_sib, 0, 0, 1)
            near_far = along_queue(far, 0, 0, 1)
            if step > 0:
                near_far, x = lax.optimization_barrier((near_far, x))
        with jax.named_scope("mix"):
            product = mix(place, o_own, far, o_near, near_far, w_out)
        with jax.named_scope("scatter"):
            parts = scatter_blocks(product)
        shape = latent.shape
        if step < STEPS - 1:
            with jax.named_scope("update"):
                speed, state, normed = update(middle_kernel, "middle", x, mods, fresh, parts, [shape] * 3)
            with jax.named_scope("gather"):
                blocks = [one_down(normed, 0, 0)] + gather_blocks(normed, one_down)
                held = lax.optimization_barrier((w_key, w_value, w_query, normed))
                weights = load(held[:3])
        else:
            speeds, new = update(last_kernel, "last", x, mods, speed, parts, [(2, *shape), shape])
    return (speeds, new)


def solution(mesh):
    return jax.shard_map(
        on_device,
        mesh=mesh,
        in_specs=(
            P(("queue", "head"), None),
            P("head", None),
            P(),
            P(),
            P(),
            P(),
            P(None, "head"),
            P(None, "head"),
            P(None, "head"),
            P("head", None),
            P("head"),
            P("head"),
        ),
        out_specs=(P(None, ("queue", "head"), None), P(("queue", "head"), None)),
        check_vma=False,
    )
```

```python
import functools
import math

import jax
import jax.numpy as jnp
from jax import lax
from jax.experimental import pallas as pl
from jax.experimental.pallas import tpu as pltpu
from jax.sharding import PartitionSpec as P

HD = 128
STEPS = 2
EXTRA = 16
F32, BF16 = jnp.float32, jnp.bfloat16
MIB = 1 << 20
VMEM_LIMIT = 8 * MIB
ALL_VMEM = 60 * MIB
LOAD_VMEM = 36 * MIB
MIX_VMEM = 48 * MIB
MIX_PARTS = 4


def along_head(array, dx, dy):
    pairs = [(y * 4 + x, ((y + dy) % 2) * 4 + (x + dx) % 4) for y in range(2) for x in range(4)]
    return lax.ppermute(array, "head", pairs)


def along_queue(array, ds, dz, dc):
    pairs = [
        (s * 8 + z * 2 + c, ((s + ds) % 2) * 8 + ((z + dz) % 4) * 2 + (c + dc) % 2)
        for s in range(2)
        for z in range(4)
        for c in range(2)
    ]
    return lax.ppermute(array, "queue", pairs)


def dot(a, b, lhs=1, rhs=0):
    return lax.dot_general(a, b, (((lhs,), (rhs,)), ((), ())), preferred_element_type=F32)


def load_kernel(*refs):
    count = len(refs) // 2
    sources, outs, arrived = refs[:count], refs[count : 2 * count], refs[-1]
    copies = [pltpu.make_async_copy(a, b, arrived.at[i]) for i, (a, b) in enumerate(zip(sources, outs))]
    for copy in copies:
        copy.start()
    for copy in copies:
        copy.wait()


def load(arrays):
    return pl.pallas_call(
        load_kernel,
        in_specs=[pl.BlockSpec(memory_space=pl.ANY)] * len(arrays),
        out_specs=[pl.BlockSpec(memory_space=pltpu.VMEM)] * len(arrays),
        out_shape=[jax.ShapeDtypeStruct(array.shape, array.dtype) for array in arrays],
        scratch_shapes=[pltpu.SemaphoreType.DMA((len(arrays),))],
        compiler_params=pltpu.CompilerParams(vmem_limit_bytes=LOAD_VMEM),
        cost_estimate=pl.CostEstimate(
            flops=0, bytes_accessed=sum(2 * array.size for array in arrays), transcendentals=0
        ),
        name="load",
    )(*arrays)


def project_kernel(place, *refs):
    blocks, weights, gains, (keep, send, rows, extra) = refs[:8], refs[8:11], refs[11], refs[12:]
    side, core = place[0], place[1]
    step, count = blocks[0].shape[0], rows.shape[0]
    for i, block in enumerate(blocks):
        rows[i * step : (i + 1) * step] = block[...]
    squares = {}
    for kind, w in enumerate(weights):
        part = dot(rows[...], w[...])
        if kind != 1:
            tiles = [part[:, i : i + HD] for i in range(0, part.shape[1], HD)]
            squares[kind] = sum(tile * tile for tile in tiles)
            part = part * gains[kind // 2 : kind // 2 + 1]
        part = part.astype(BF16)
        for pair in range(2):
            first, second = (part[:, (2 * pair + i) * HD : (2 * pair + i + 1) * HD] for i in range(2))
            at = jnp.where(side == pair, 0, 3) + kind
            to = pl.ds(pl.multiple_of(at * count, count), count)

            @pl.when(core == 0)
            def _():
                keep[to, :] = first
                send[to, :] = second

            @pl.when(core == 1)
            def _():
                keep[to, :] = second
                send[to, :] = first

    for i, kind in enumerate((2, 0)):
        for half in range(2):
            line = jnp.sum(squares[kind][half * HD : (half + 1) * HD].T, axis=0, keepdims=True)
            high = line.astype(BF16).astype(F32)
            at = i * 2 + half
            extra[at : at + 1] = high
            extra[8 + at : 9 + at] = line - high
    for at in (4, 12):
        extra[at : at + 4] = jnp.zeros((4, HD), F32)
    keep[6 * count :] = extra[...].astype(BF16)
    send[6 * count :] = extra[...].astype(BF16)


def project(place, blocks, wk, wv, wq, gains):
    block_rows, depth = blocks[0].shape
    rows, n = 8 * block_rows, wq.shape[1]
    out = jax.ShapeDtypeStruct((6 * rows + EXTRA, HD), BF16)
    vmem = pl.BlockSpec(memory_space=pltpu.VMEM)
    return pl.pallas_call(
        project_kernel,
        in_specs=[pl.BlockSpec(memory_space=pltpu.SMEM)] + [vmem] * 12,
        out_specs=[vmem] * 2,
        out_shape=[out, out],
        scratch_shapes=[pltpu.VMEM((rows, depth), BF16), pltpu.VMEM((EXTRA, HD), F32)],
        compiler_params=pltpu.CompilerParams(vmem_limit_bytes=VMEM_LIMIT),
        cost_estimate=pl.CostEstimate(
            flops=6 * rows * depth * n, bytes_accessed=6 * depth * n, transcendentals=0
        ),
        name="project",
    )(place, *blocks, wk, wv, wq, gains)


def assemble_kernel(keep, swapped, near, far, far_queries, sums):
    count = near.shape[0] // 4
    for i, ref in enumerate((keep, swapped)):
        near[2 * i * count : 2 * (i + 1) * count] = ref[: 2 * count]
        far[2 * i * count : 2 * (i + 1) * count] = ref[3 * count : 5 * count]
        far_queries[i * count : (i + 1) * count] = ref[5 * count : 6 * count]
        extra = ref[6 * count :].astype(F32)
        sums[4 * i : 4 * (i + 1)] = extra[:4] + extra[8:12]


def assemble(keep, swapped):
    vmem = pl.BlockSpec(memory_space=pltpu.VMEM)
    rows = (keep.shape[0] - EXTRA) // 6
    return pl.pallas_call(
        assemble_kernel,
        in_specs=[vmem] * 2,
        out_specs=[vmem] * 4,
        out_shape=[
            jax.ShapeDtypeStruct((4 * rows, HD), BF16),
            jax.ShapeDtypeStruct((4 * rows, HD), BF16),
            jax.ShapeDtypeStruct((2 * rows, HD), BF16),
            jax.ShapeDtypeStruct((8, HD), F32),
        ],
        compiler_params=pltpu.CompilerParams(vmem_limit_bytes=VMEM_LIMIT),
        name="assemble",
    )(keep, swapped)


def in_two(sums):
    high = sums.astype(BF16).astype(F32)
    return jnp.concatenate([high, sums - high], axis=0).astype(BF16)


def from_two(lines):
    lines = lines.astype(F32)
    return lines[:8] + lines[8:]


def append_kernel(sums, other, near, far, total, near_out, far_out):
    values, line = other[...], lax.broadcasted_iota(jnp.int32, other.shape, 0)
    up, down = jnp.concatenate([values[1:], values[:1]], axis=0), jnp.concatenate([values[7:], values[:7]], axis=0)
    values = sums[...] + jnp.where(line % 2 == 0, up, down)
    total[...] = values
    count = near.shape[0]
    for ref, out in ((near, near_out), (far, far_out)):
        out[:count] = ref[...]
        out[count:] = in_two(values)


def append_sums(sums, other, near, far):
    vmem = pl.BlockSpec(memory_space=pltpu.VMEM)
    longer = jax.ShapeDtypeStruct((near.shape[0] + EXTRA, HD), BF16)
    return pl.pallas_call(
        append_kernel,
        in_specs=[vmem] * 4,
        out_specs=[vmem] * 3,
        out_shape=[jax.ShapeDtypeStruct(sums.shape, F32), longer, longer],
        compiler_params=pltpu.CompilerParams(vmem_limit_bytes=VMEM_LIMIT),
        name="append",
    )(sums, other, near, far)


def collect_kernel(queries, *refs):
    arrays, out = refs[:-1], refs[-1]
    count = queries.shape[0]
    out[:count] = queries[...]
    for i, ref in enumerate(arrays):
        out[count + i * EXTRA : count + (i + 1) * EXTRA] = ref[ref.shape[0] - EXTRA :]


def collect_sums(queries, arrays):
    vmem = pl.BlockSpec(memory_space=pltpu.VMEM)
    return pl.pallas_call(
        collect_kernel,
        in_specs=[vmem] * (1 + len(arrays)),
        out_specs=vmem,
        out_shape=jax.ShapeDtypeStruct((queries.shape[0] + len(arrays) * EXTRA, HD), BF16),
        compiler_params=pltpu.CompilerParams(vmem_limit_bytes=VMEM_LIMIT),
        name="collect",
    )(queries, *arrays)


def row_scales(lines, every):
    scales = lax.rsqrt(lines * (1.0 / every) + 1e-6)
    return jnp.concatenate([scales, jnp.zeros((HD - lines.shape[0], HD), F32)], axis=0).T


def scale_column(scales, span, kind):
    at = 4 * span + 2 * kind
    return jnp.concatenate([scales[:, at : at + 1], scales[:, at + 1 : at + 2]], axis=0)


def attend_span(queries, scale, lower, slot, keys, values):
    rows = queries.shape[0]
    queries = (queries.astype(F32) * scale).astype(BF16)

    def absorb(width):
        def block(j, carry):
            top, total, acc = carry
            part = pl.ds(pl.multiple_of(j * rows, rows), width * rows)
            scores = dot(keys[part, :], queries, 1, 1)
            new_top = jnp.maximum(top, jnp.max(scores, axis=0, keepdims=True))
            weights = jnp.exp2(scores - new_top)
            fade = jnp.exp2(top - new_top)
            total = total * fade + jnp.sum(weights, axis=0, keepdims=True)
            acc = acc * fade + dot(values[part, :], weights.astype(BF16), 0, 0)
            return new_top, total, acc

        return block

    carry = (
        jnp.full((1, rows), -1e30, F32),
        jnp.zeros((1, rows), F32),
        jnp.zeros((HD, rows), F32),
    )
    count = slot + 1 - lower
    at = lower
    for width in WIDTHS:
        times = count // width
        carry = lax.fori_loop(0, times, lambda i, c, w=width, a=at: absorb(w)(a + i * w, c), carry)
        at, count = at + times * width, count - times * width
    _, total, acc = carry
    return (acc / total).T.astype(BF16)


LOG2_SCALE = math.log2(math.e) / math.sqrt(HD)
WIDTHS = (8, 4, 2, 1)


def attend_far_kernel(every, place, *refs):
    pairs, queries, (out, keys, values) = refs[:8], refs[8], refs[9:]
    rows = out.shape[1]
    behind = [pairs[i][4 * rows :] for i in (0, 5, 2, 7)]
    near_scales = row_scales(jnp.concatenate([from_two(lines) for lines in behind], axis=0), every)
    behind = [queries[2 * rows + i * EXTRA : 2 * rows + (i + 1) * EXTRA] for i in range(4)]
    far_scales = row_scales(jnp.concatenate([from_two(lines) for lines in behind], axis=0), every)
    for at in range(16):
        scales = far_scales if at % 4 // 2 else near_scales
        ref, first = pairs[at // 4 + 4 * (at % 4 // 2)], 2 * (at % 2) * rows
        to = pl.ds(pl.multiple_of(place[8 + at] * rows, rows), rows)
        scale = scale_column(scales, 2 * (at // 4) + at % 2, 1)
        keys[to, :] = (ref[first : first + rows].astype(F32) * scale).astype(BF16)
        values[to, :] = ref[first + rows : first + 2 * rows]
    for span in range(2):
        out[span] = attend_span(
            queries[span * rows : (span + 1) * rows],
            scale_column(far_scales, span, 0) * LOG2_SCALE,
            place[6 + span],
            place[2 + span],
            keys,
            values,
        )


def attend_near_kernel(every, place, sums, keep, swapped, keys, values, out_own, out_sib):
    rows = out_own.shape[0]
    scales = row_scales(sums[...], every)
    for span, (queries, out) in enumerate(((keep, out_own), (swapped, out_sib))):
        out[...] = attend_span(
            queries[2 * rows : 3 * rows],
            scale_column(scales, span, 0) * LOG2_SCALE,
            place[4 + span],
            place[span],
            keys,
            values,
        )


def attend_cost(rows):
    return pl.CostEstimate(flops=4 * 16 * rows * rows * HD, bytes_accessed=2 * MIB, transcendentals=16 * rows * rows)


def attend_far(place, pairs, queries, every):
    rows = pairs[1].shape[0] // 4
    vmem, smem = pl.BlockSpec(memory_space=pltpu.VMEM), pl.BlockSpec(memory_space=pltpu.SMEM)
    spans = jax.ShapeDtypeStruct((16 * rows, HD), BF16)
    return pl.pallas_call(
        functools.partial(attend_far_kernel, every),
        in_specs=[smem] + [vmem] * 9,
        out_specs=[vmem] * 3,
        out_shape=[jax.ShapeDtypeStruct((2, rows, HD), BF16), spans, spans],
        compiler_params=pltpu.CompilerParams(vmem_limit_bytes=VMEM_LIMIT),
        cost_estimate=attend_cost(rows),
        name="attend_far",
    )(place, *pairs, queries)


def attend_near(place, sums, keep, swapped, keys, values, every):
    rows = keys.shape[0] // 16
    vmem, smem = pl.BlockSpec(memory_space=pltpu.VMEM), pl.BlockSpec(memory_space=pltpu.SMEM)
    out = jax.ShapeDtypeStruct((rows, HD), BF16)
    return pl.pallas_call(
        functools.partial(attend_near_kernel, every),
        in_specs=[smem] + [vmem] * 5,
        out_specs=[vmem] * 2,
        out_shape=[out, out],
        compiler_params=pltpu.CompilerParams(vmem_limit_bytes=VMEM_LIMIT),
        cost_estimate=attend_cost(rows),
        name="attend_near",
    )(place, sums, keep, swapped, keys, values)


def mix_kernel(place, own, far, near, near_far, w, *refs):
    outs, (acts, held, arrived) = refs[:8], refs[8:]
    part = w.shape[0] // MIX_PARTS
    parts = [pl.ds(i * part, part) for i in range(MIX_PARTS)]
    copies = [pltpu.make_async_copy(w.at[at], held.at[at], arrived.at[i]) for i, at in enumerate(parts)]
    for copy in copies:
        copy.start()
    side, core = place[0], place[1]
    for values, s, c in (
        (own[...], side, core),
        (far[0], 1 - side, core),
        (near[...], side, 1 - core),
        (near_far[1], 1 - side, 1 - core),
    ):
        acts[:, pl.ds(pl.multiple_of((2 * s + c) * HD, HD), HD)] = values
    for copy in copies:
        copy.wait()
    step, width, tile = acts.shape[0] // 8, w.shape[1], 512
    for i in range(0, width, tile):
        product = dot(acts[...], held[:, i : i + tile]).astype(BF16)
        for at, out in enumerate(outs):
            out[:, i : i + tile] = product[at * step : (at + 1) * step]


def mix(place, own, far, near, near_far, w):
    rows, depth, width = own.shape[0], w.shape[0], w.shape[1]
    vmem = pl.BlockSpec(memory_space=pltpu.VMEM)
    return pl.pallas_call(
        mix_kernel,
        in_specs=[pl.BlockSpec(memory_space=pltpu.SMEM)] + [vmem] * 4 + [pl.BlockSpec(memory_space=pl.ANY)],
        out_specs=[vmem] * 8,
        out_shape=[jax.ShapeDtypeStruct((rows // 8, width), BF16)] * 8,
        scratch_shapes=[
            pltpu.VMEM((rows, depth), BF16),
            pltpu.VMEM(w.shape, BF16),
            pltpu.SemaphoreType.DMA((MIX_PARTS,)),
        ],
        compiler_params=pltpu.CompilerParams(vmem_limit_bytes=MIX_VMEM),
        cost_estimate=pl.CostEstimate(
            flops=2 * rows * depth * width, bytes_accessed=2 * depth * width, transcendentals=0
        ),
        name="mix",
    )(place, own, far, near, near_far, w)


def norm_rows(x, scale, shift):
    mean = jnp.mean(x, axis=-1, keepdims=True)
    var = jnp.mean((x - mean) ** 2, axis=-1, keepdims=True)
    return ((x - mean) * lax.rsqrt(var + 1e-06) * (1.0 + scale) + shift).astype(BF16)


def start_kernel(place, levels_at, plan_at, x_at, table_at, out, mods, levels, plan, x, table, arrived):
    pairs = ((levels_at, levels), (plan_at, plan), (table_at, table), (x_at, x))
    copies = [pltpu.make_async_copy(a, b, arrived.at[i]) for i, (a, b) in enumerate(pairs)]
    for copy in copies:
        copy.start()
    half = table.shape[1] // 2
    at = lax.broadcasted_iota(jnp.int32, (8, half), 1).astype(F32)
    freq = jnp.exp(-math.log(10000.0) * at / half)
    line = lax.broadcasted_iota(jnp.int32, (8, half), 0)
    for copy in copies:
        copy.wait()
    slot = place[2]
    t_from, t_below = (plan[levels[place[2 + i]]].astype(F32) for i in range(2))
    angle = jnp.where(line < 3, t_from, t_below) * freq
    emb = jnp.concatenate([jnp.cos(angle), jnp.sin(angle)], axis=1)
    values = table[...]
    mods[...] = jnp.concatenate([values, values[:2], values], axis=0) + emb
    mods[5:6] = jnp.full((1, 2 * half), (jnp.where(slot > 0, t_below, 0.0) - t_from) / 1000.0, F32)
    mods[6:7] = jnp.full((1, 2 * half), jnp.where(slot == 0, 1.0, 0.0), F32)
    out[...] = norm_rows(x[...].astype(F32), mods[1:2], mods[0:1])


def start(place, levels, plan, x, table):
    vmem, smem = pl.BlockSpec(memory_space=pltpu.VMEM), pl.BlockSpec(memory_space=pltpu.SMEM)
    hbm = pl.BlockSpec(memory_space=pl.ANY)
    return pl.pallas_call(
        start_kernel,
        in_specs=[smem] + [hbm] * 4,
        out_specs=[vmem] * 2,
        out_shape=[jax.ShapeDtypeStruct(x.shape, BF16), jax.ShapeDtypeStruct((8, x.shape[1]), F32)],
        scratch_shapes=[
            pltpu.SMEM(levels.shape, jnp.int32),
            pltpu.SMEM(plan.shape, jnp.int32),
            pltpu.VMEM(x.shape, BF16),
            pltpu.VMEM(table.shape, F32),
            pltpu.SemaphoreType.DMA((4,)),
        ],
        compiler_params=pltpu.CompilerParams(vmem_limit_bytes=ALL_VMEM),
        name="start",
    )(place, levels, plan, x, table)


def stepped(x, mods, parts):
    mixed = parts[0][...].astype(F32)
    for part in parts[1:]:
        mixed += part[...].astype(F32)
    x = x[...].astype(F32)
    speed = (x + mods[2:3] * mixed).astype(BF16)
    return speed, (x + mods[5:6] * speed.astype(F32)).astype(BF16)


def middle_kernel(x, mods, fresh, *refs):
    parts, (speed_out, state_out, normed_out) = refs[:-3], refs[-3:]
    speed, new = stepped(x, mods, parts)
    speed_out[...] = speed
    state = jnp.where(mods[6:7] > 0.5, fresh[...].astype(F32), new.astype(F32))
    state_out[...] = state.astype(BF16)
    normed_out[...] = norm_rows(state, mods[4:5], mods[3:4])


def last_kernel(x, mods, before, *refs):
    parts, (speeds_out, new_out) = refs[:-2], refs[-2:]
    speed, new = stepped(x, mods, parts)
    speeds_out[0] = before[...]
    speeds_out[1] = speed
    new_out[...] = new


def update(kernel, name, x, mods, other, parts, shapes):
    vmem = pl.BlockSpec(memory_space=pltpu.VMEM)
    return pl.pallas_call(
        kernel,
        in_specs=[vmem] * (3 + len(parts)),
        out_specs=[vmem] * len(shapes),
        out_shape=[jax.ShapeDtypeStruct(shape, BF16) for shape in shapes],
        compiler_params=pltpu.CompilerParams(vmem_limit_bytes=VMEM_LIMIT),
        name=name,
    )(x, mods, other, *parts)


def one_down(array, dx, dy):
    queue = lax.axis_size("queue")
    pairs = [
        (q * 8 + y * 4 + x, ((q - 1) % queue) * 8 + ((y + dy) % 2) * 4 + (x + dx) % 4)
        for q in range(queue)
        for y in range(2)
        for x in range(4)
    ]
    return lax.ppermute(array, ("queue", "head"), pairs)


def gather_blocks(block, move):
    other = move(block, 0, 1)
    left, right, across = move(block, 1, 0), move(block, -1, 0), move(block, 2, 0)
    other_left, other_right = along_head(other, 1, 0), along_head(other, -1, 0)
    other_across = along_head(across, 0, 1)
    return [right, across, left, other, other_right, other_across, other_left]


def scatter_blocks(blocks):
    own, right, across, left, other, other_right, other_across, other_left = blocks
    add = lambda *terms: sum(term.astype(F32) for term in terms).astype(BF16)
    from_left, from_right = along_head(other_right, 1, 0), along_head(other_left, -1, 0)
    from_other = along_head(other_across, 0, 1)
    gets = [along_head(right, 1, 0), along_head(left, -1, 0)]
    gets.append(along_head(add(other, from_left, from_right), 0, 1))
    gets.append(along_head(add(across, from_other), 2, 0))
    return [own] + gets


def turned(sums, by):
    by *= HD // 4
    return jnp.concatenate([sums[:, by:], sums[:, :by]], axis=1)


def on_device(
    latent, fresh, levels, windows, plan, mod_table, w_query, w_key, w_value, w_out, query_gain, key_gain
):
    queue_count, head_count = lax.axis_size("queue"), lax.axis_size("head")
    slot = lax.axis_index("queue")
    rows = latent.shape[0]
    span = rows * head_count
    every = w_query.shape[1] * head_count
    side, z, core = slot // 8, (slot // 2) % 4, slot % 2
    place = jnp.stack([side, core, slot, (slot + queue_count - 1) % queue_count])
    places = jnp.stack(
        [
            ((side + s) % 2) * 8 + ((z + dz) % 4) * 2 + (core + c) % 2
            for dz in range(4)
            for s in range(2)
            for c in range(2)
        ]
    )
    lowers = jnp.maximum(0, jnp.arange(queue_count, dtype=jnp.int32) - windows + 1)
    order = jnp.concatenate([places[:4], lowers[places[:4]], places])

    gains = jnp.stack([key_gain, query_gain])

    x = latent
    normed, mods = start(place, levels, plan, x, mod_table)
    blocks = [normed] + gather_blocks(normed, along_head)
    weights = load([w_key, w_value, w_query])
    for step in range(STEPS):
        with jax.named_scope("project"):
            keep, send = project(place, blocks, *weights, gains)
        with jax.named_scope("swap"):
            swapped = along_queue(send, 0, 0, 1)
            near, far, queries, sums = assemble(keep, swapped)
        with jax.named_scope("round1"):
            near1, near3 = along_queue(near, 0, -1, 0), along_queue(near, 0, 1, 0)
            far = along_queue(far, 1, 0, 0)
            others = [along_head(sums, by, 0) for by in (1, 2, 3)]
            near1, near3, far, others = lax.optimization_barrier((near1, near3, far, others))
            for by in (1, 2, 3):
                sums += turned(others[by - 1], by)
        with jax.named_scope("round2"):
            other = along_head(sums, 0, 1)
            sums, near, far = append_sums(sums, other, near, far)
        with jax.named_scope("round3"):
            far1, far3 = along_queue(far, 0, -1, 0), along_queue(far, 0, 1, 0)
            near2 = along_queue(near, 0, -2, 0)
        with jax.named_scope("round4"):
            queries = collect_sums(queries, [near, far1, near2, far3])
            queries = along_queue(queries, 1, 0, 0)
            far2 = along_queue(far, 0, -2, 0)
        with jax.named_scope("attend"):
            if step > 0:
                state, queries = lax.optimization_barrier((state, queries))
                x = one_down(state, 0, 0)
            pairs = [near, near1, near2, near3, far, far1, far2, far3]
            o_far, keys, values = attend_far(order, pairs, queries, every)
            far = along_queue(o_far, 1, 0, 0)
            o_own, o_sib = attend_near(order, sums, keep, swapped, keys, values, every)
            far, o_sib = lax.optimization_barrier((far, o_sib))
            o_near = along_queue(o_sib, 0, 0, 1)
            near_far = along_queue(far, 0, 0, 1)
            if step > 0:
                near_far, x = lax.optimization_barrier((near_far, x))
        with jax.named_scope("mix"):
            product = mix(place, o_own, far, o_near, near_far, w_out)
        with jax.named_scope("scatter"):
            parts = scatter_blocks(product)
        shape = latent.shape
        if step < STEPS - 1:
            with jax.named_scope("update"):
                speed, state, normed = update(middle_kernel, "middle", x, mods, fresh, parts, [shape] * 3)
            with jax.named_scope("gather"):
                blocks = [one_down(normed, 0, 0)] + gather_blocks(normed, one_down)
                held = lax.optimization_barrier((w_key, w_value, w_query, normed))
                weights = load(held[:3])
        else:
            speeds, new = update(last_kernel, "last", x, mods, speed, parts, [(2, *shape), shape])
    return (speeds, new)


def solution(mesh):
    return jax.shard_map(
        on_device,
        mesh=mesh,
        in_specs=(
            P(("queue", "head"), None),
            P("head", None),
            P(),
            P(),
            P(),
            P(),
            P(None, "head"),
            P(None, "head"),
            P(None, "head"),
            P("head", None),
            P("head"),
            P("head"),
        ),
        out_specs=(P(None, ("queue", "head"), None), P(("queue", "head"), None)),
        check_vma=False,
    )
```

```python
import functools
import math

import jax
import jax.numpy as jnp
from jax import lax
from jax.experimental import pallas as pl
from jax.experimental.pallas import tpu as pltpu
from jax.sharding import PartitionSpec as P

HD = 128
STEPS = 2
EXTRA = 16
F32, BF16 = jnp.float32, jnp.bfloat16
MIB = 1 << 20
VMEM_LIMIT = 8 * MIB
ALL_VMEM = 60 * MIB
LOAD_VMEM = 36 * MIB
FAR_VMEM = 42 * MIB


def along_head(array, dx, dy):
    pairs = [(y * 4 + x, ((y + dy) % 2) * 4 + (x + dx) % 4) for y in range(2) for x in range(4)]
    return lax.ppermute(array, "head", pairs)


def along_queue(array, ds, dz, dc):
    pairs = [
        (s * 8 + z * 2 + c, ((s + ds) % 2) * 8 + ((z + dz) % 4) * 2 + (c + dc) % 2)
        for s in range(2)
        for z in range(4)
        for c in range(2)
    ]
    return lax.ppermute(array, "queue", pairs)


def dot(a, b, lhs=1, rhs=0):
    return lax.dot_general(a, b, (((lhs,), (rhs,)), ((), ())), preferred_element_type=F32)


def load_kernel(*refs):
    count = len(refs) // 2
    sources, outs, arrived = refs[:count], refs[count : 2 * count], refs[-1]
    copies = [pltpu.make_async_copy(a, b, arrived.at[i]) for i, (a, b) in enumerate(zip(sources, outs))]
    for copy in copies:
        copy.start()
    for copy in copies:
        copy.wait()


def load(arrays):
    return pl.pallas_call(
        load_kernel,
        in_specs=[pl.BlockSpec(memory_space=pl.ANY)] * len(arrays),
        out_specs=[pl.BlockSpec(memory_space=pltpu.VMEM)] * len(arrays),
        out_shape=[jax.ShapeDtypeStruct(array.shape, array.dtype) for array in arrays],
        scratch_shapes=[pltpu.SemaphoreType.DMA((len(arrays),))],
        compiler_params=pltpu.CompilerParams(vmem_limit_bytes=LOAD_VMEM),
        cost_estimate=pl.CostEstimate(
            flops=0, bytes_accessed=sum(2 * array.size for array in arrays), transcendentals=0
        ),
        name="load",
    )(*arrays)


def project_kernel(place, *refs):
    blocks, weights, gains, (keep, send, rows, extra) = refs[:8], refs[8:11], refs[11], refs[12:]
    side, core = place[0], place[1]
    step, count = blocks[0].shape[0], rows.shape[0]
    for i, block in enumerate(blocks):
        rows[i * step : (i + 1) * step] = block[...]
    squares = {}
    for kind, w in enumerate(weights):
        part = dot(rows[...], w[...])
        if kind != 1:
            tiles = [part[:, i : i + HD] for i in range(0, part.shape[1], HD)]
            squares[kind] = sum(tile * tile for tile in tiles)
            part = part * gains[kind // 2 : kind // 2 + 1]
        part = part.astype(BF16)
        for pair in range(2):
            first, second = (part[:, (2 * pair + i) * HD : (2 * pair + i + 1) * HD] for i in range(2))
            at = jnp.where(side == pair, 0, 3) + kind
            to = pl.ds(pl.multiple_of(at * count, count), count)

            @pl.when(core == 0)
            def _():
                keep[to, :] = first
                send[to, :] = second

            @pl.when(core == 1)
            def _():
                keep[to, :] = second
                send[to, :] = first

    for i, kind in enumerate((2, 0)):
        for half in range(2):
            line = jnp.sum(squares[kind][half * HD : (half + 1) * HD].T, axis=0, keepdims=True)
            high = line.astype(BF16).astype(F32)
            at = i * 2 + half
            extra[at : at + 1] = high
            extra[8 + at : 9 + at] = line - high
    for at in (4, 12):
        extra[at : at + 4] = jnp.zeros((4, HD), F32)
    keep[6 * count :] = extra[...].astype(BF16)
    send[6 * count :] = extra[...].astype(BF16)


def project(place, blocks, wk, wv, wq, gains):
    block_rows, depth = blocks[0].shape
    rows, n = 8 * block_rows, wq.shape[1]
    out = jax.ShapeDtypeStruct((6 * rows + EXTRA, HD), BF16)
    vmem = pl.BlockSpec(memory_space=pltpu.VMEM)
    return pl.pallas_call(
        project_kernel,
        in_specs=[pl.BlockSpec(memory_space=pltpu.SMEM)] + [vmem] * 12,
        out_specs=[vmem] * 2,
        out_shape=[out, out],
        scratch_shapes=[pltpu.VMEM((rows, depth), BF16), pltpu.VMEM((EXTRA, HD), F32)],
        compiler_params=pltpu.CompilerParams(vmem_limit_bytes=VMEM_LIMIT),
        cost_estimate=pl.CostEstimate(
            flops=6 * rows * depth * n, bytes_accessed=6 * depth * n, transcendentals=0
        ),
        name="project",
    )(place, *blocks, wk, wv, wq, gains)


def assemble_kernel(keep, swapped, near, far, far_queries, sums):
    count = near.shape[0] // 4
    for i, ref in enumerate((keep, swapped)):
        near[2 * i * count : 2 * (i + 1) * count] = ref[: 2 * count]
        far[2 * i * count : 2 * (i + 1) * count] = ref[3 * count : 5 * count]
        far_queries[i * count : (i + 1) * count] = ref[5 * count : 6 * count]
        extra = ref[6 * count :].astype(F32)
        sums[4 * i : 4 * (i + 1)] = extra[:4] + extra[8:12]


def assemble(keep, swapped):
    vmem = pl.BlockSpec(memory_space=pltpu.VMEM)
    rows = (keep.shape[0] - EXTRA) // 6
    return pl.pallas_call(
        assemble_kernel,
        in_specs=[vmem] * 2,
        out_specs=[vmem] * 4,
        out_shape=[
            jax.ShapeDtypeStruct((4 * rows, HD), BF16),
            jax.ShapeDtypeStruct((4 * rows, HD), BF16),
            jax.ShapeDtypeStruct((2 * rows, HD), BF16),
            jax.ShapeDtypeStruct((8, HD), F32),
        ],
        compiler_params=pltpu.CompilerParams(vmem_limit_bytes=VMEM_LIMIT),
        name="assemble",
    )(keep, swapped)


def in_two(sums):
    high = sums.astype(BF16).astype(F32)
    return jnp.concatenate([high, sums - high], axis=0).astype(BF16)


def from_two(lines):
    lines = lines.astype(F32)
    return lines[:8] + lines[8:]


def append_kernel(sums, other, near, far, total, near_out, far_out):
    values, line = other[...], lax.broadcasted_iota(jnp.int32, other.shape, 0)
    up, down = jnp.concatenate([values[1:], values[:1]], axis=0), jnp.concatenate([values[7:], values[:7]], axis=0)
    values = sums[...] + jnp.where(line % 2 == 0, up, down)
    total[...] = values
    count = near.shape[0]
    for ref, out in ((near, near_out), (far, far_out)):
        out[:count] = ref[...]
        out[count:] = in_two(values)


def append_sums(sums, other, near, far):
    vmem = pl.BlockSpec(memory_space=pltpu.VMEM)
    longer = jax.ShapeDtypeStruct((near.shape[0] + EXTRA, HD), BF16)
    return pl.pallas_call(
        append_kernel,
        in_specs=[vmem] * 4,
        out_specs=[vmem] * 3,
        out_shape=[jax.ShapeDtypeStruct(sums.shape, F32), longer, longer],
        compiler_params=pltpu.CompilerParams(vmem_limit_bytes=VMEM_LIMIT),
        name="append",
    )(sums, other, near, far)


def collect_kernel(queries, *refs):
    arrays, out = refs[:-1], refs[-1]
    count = queries.shape[0]
    out[:count] = queries[...]
    for i, ref in enumerate(arrays):
        out[count + i * EXTRA : count + (i + 1) * EXTRA] = ref[ref.shape[0] - EXTRA :]


def collect_sums(queries, arrays):
    vmem = pl.BlockSpec(memory_space=pltpu.VMEM)
    return pl.pallas_call(
        collect_kernel,
        in_specs=[vmem] * (1 + len(arrays)),
        out_specs=vmem,
        out_shape=jax.ShapeDtypeStruct((queries.shape[0] + len(arrays) * EXTRA, HD), BF16),
        compiler_params=pltpu.CompilerParams(vmem_limit_bytes=VMEM_LIMIT),
        name="collect",
    )(queries, *arrays)


def row_scales(lines, every):
    scales = lax.rsqrt(lines * (1.0 / every) + 1e-6)
    return jnp.concatenate([scales, jnp.zeros((HD - lines.shape[0], HD), F32)], axis=0).T


def scale_column(scales, span, kind):
    at = 4 * span + 2 * kind
    return jnp.concatenate([scales[:, at : at + 1], scales[:, at + 1 : at + 2]], axis=0)


def attend_span(queries, scale, lower, slot, keys, values):
    rows = queries.shape[0]
    queries = (queries.astype(F32) * scale).astype(BF16)

    def absorb(width):
        def block(j, carry):
            top, total, acc = carry
            part = pl.ds(pl.multiple_of(j * rows, rows), width * rows)
            scores = dot(keys[part, :], queries, 1, 1)
            new_top = jnp.maximum(top, jnp.max(scores, axis=0, keepdims=True))
            weights = jnp.exp2(scores - new_top)
            fade = jnp.exp2(top - new_top)
            total = total * fade + jnp.sum(weights, axis=0, keepdims=True)
            acc = acc * fade + dot(values[part, :], weights.astype(BF16), 0, 0)
            return new_top, total, acc

        return block

    carry = (
        jnp.full((1, rows), -1e30, F32),
        jnp.zeros((1, rows), F32),
        jnp.zeros((HD, rows), F32),
    )
    count = slot + 1 - lower
    at = lower
    for width in WIDTHS:
        times = count // width
        carry = lax.fori_loop(0, times, lambda i, c, w=width, a=at: absorb(w)(a + i * w, c), carry)
        at, count = at + times * width, count - times * width
    _, total, acc = carry
    return (acc / total).T.astype(BF16)


LOG2_SCALE = math.log2(math.e) / math.sqrt(HD)
WIDTHS = (8, 4, 2, 1)


def attend_far_kernel(every, place, *refs):
    pairs, queries, w, (out, keys, values, w_near, arrived) = refs[:8], refs[8], refs[9], refs[10:]
    part = w.shape[0] // 4
    parts = [pl.ds(i * part, part) for i in range(4)]
    copies = [pltpu.make_async_copy(w.at[at], w_near.at[at], arrived.at[i]) for i, at in enumerate(parts)]
    for copy in copies:
        copy.start()
    rows = out.shape[1]
    behind = [pairs[i][4 * rows :] for i in (0, 5, 2, 7)]
    near_scales = row_scales(jnp.concatenate([from_two(lines) for lines in behind], axis=0), every)
    behind = [queries[2 * rows + i * EXTRA : 2 * rows + (i + 1) * EXTRA] for i in range(4)]
    far_scales = row_scales(jnp.concatenate([from_two(lines) for lines in behind], axis=0), every)
    for at in range(16):
        scales = far_scales if at % 4 // 2 else near_scales
        ref, first = pairs[at // 4 + 4 * (at % 4 // 2)], 2 * (at % 2) * rows
        to = pl.ds(pl.multiple_of(place[8 + at] * rows, rows), rows)
        scale = scale_column(scales, 2 * (at // 4) + at % 2, 1)
        keys[to, :] = (ref[first : first + rows].astype(F32) * scale).astype(BF16)
        values[to, :] = ref[first + rows : first + 2 * rows]
    for span in range(2):
        out[span] = attend_span(
            queries[span * rows : (span + 1) * rows],
            scale_column(far_scales, span, 0) * LOG2_SCALE,
            place[6 + span],
            place[2 + span],
            keys,
            values,
        )
    for copy in copies:
        copy.wait()


def attend_near_kernel(every, place, sums, keep, swapped, keys, values, out_own, out_sib):
    rows = out_own.shape[0]
    scales = row_scales(sums[...], every)
    for span, (queries, out) in enumerate(((keep, out_own), (swapped, out_sib))):
        out[...] = attend_span(
            queries[2 * rows : 3 * rows],
            scale_column(scales, span, 0) * LOG2_SCALE,
            place[4 + span],
            place[span],
            keys,
            values,
        )


def attend_cost(rows):
    return pl.CostEstimate(flops=4 * 16 * rows * rows * HD, bytes_accessed=2 * MIB, transcendentals=16 * rows * rows)


def attend_far(place, pairs, queries, w, every):
    rows = pairs[1].shape[0] // 4
    vmem, smem = pl.BlockSpec(memory_space=pltpu.VMEM), pl.BlockSpec(memory_space=pltpu.SMEM)
    spans = jax.ShapeDtypeStruct((16 * rows, HD), BF16)
    return pl.pallas_call(
        functools.partial(attend_far_kernel, every),
        in_specs=[smem] + [vmem] * 9 + [pl.BlockSpec(memory_space=pl.ANY)],
        out_specs=[vmem] * 4,
        out_shape=[
            jax.ShapeDtypeStruct((2, rows, HD), BF16),
            spans,
            spans,
            jax.ShapeDtypeStruct(w.shape, w.dtype),
        ],
        scratch_shapes=[pltpu.SemaphoreType.DMA((4,))],
        compiler_params=pltpu.CompilerParams(vmem_limit_bytes=FAR_VMEM),
        cost_estimate=attend_cost(rows),
        name="attend_far",
    )(place, *pairs, queries, w)


def attend_near(place, sums, keep, swapped, keys, values, every):
    rows = keys.shape[0] // 16
    vmem, smem = pl.BlockSpec(memory_space=pltpu.VMEM), pl.BlockSpec(memory_space=pltpu.SMEM)
    out = jax.ShapeDtypeStruct((rows, HD), BF16)
    return pl.pallas_call(
        functools.partial(attend_near_kernel, every),
        in_specs=[smem] + [vmem] * 5,
        out_specs=[vmem] * 2,
        out_shape=[out, out],
        compiler_params=pltpu.CompilerParams(vmem_limit_bytes=VMEM_LIMIT),
        cost_estimate=attend_cost(rows),
        name="attend_near",
    )(place, sums, keep, swapped, keys, values)


def mix_kernel(place, own, far, near, near_far, w, *refs):
    outs, acts = refs[:8], refs[8]
    side, core = place[0], place[1]
    for values, s, c in (
        (own[...], side, core),
        (far[0], 1 - side, core),
        (near[...], side, 1 - core),
        (near_far[1], 1 - side, 1 - core),
    ):
        acts[:, pl.ds(pl.multiple_of((2 * s + c) * HD, HD), HD)] = values
    step, width, tile = acts.shape[0] // 8, w.shape[1], 512
    for i in range(0, width, tile):
        product = dot(acts[...], w[:, i : i + tile]).astype(BF16)
        for at, out in enumerate(outs):
            out[:, i : i + tile] = product[at * step : (at + 1) * step]


def mix(place, own, far, near, near_far, w):
    rows, depth, width = own.shape[0], w.shape[0], w.shape[1]
    vmem = pl.BlockSpec(memory_space=pltpu.VMEM)
    return pl.pallas_call(
        mix_kernel,
        in_specs=[pl.BlockSpec(memory_space=pltpu.SMEM)] + [vmem] * 5,
        out_specs=[vmem] * 8,
        out_shape=[jax.ShapeDtypeStruct((rows // 8, width), BF16)] * 8,
        scratch_shapes=[pltpu.VMEM((rows, depth), BF16)],
        compiler_params=pltpu.CompilerParams(vmem_limit_bytes=VMEM_LIMIT),
        cost_estimate=pl.CostEstimate(
            flops=2 * rows * depth * width, bytes_accessed=2 * depth * width, transcendentals=0
        ),
        name="mix",
    )(place, own, far, near, near_far, w)


def norm_rows(x, scale, shift):
    mean = jnp.mean(x, axis=-1, keepdims=True)
    var = jnp.mean((x - mean) ** 2, axis=-1, keepdims=True)
    return ((x - mean) * lax.rsqrt(var + 1e-06) * (1.0 + scale) + shift).astype(BF16)


def start_kernel(place, levels_at, plan_at, x_at, table_at, out, mods, levels, plan, x, table, arrived):
    pairs = ((levels_at, levels), (plan_at, plan), (table_at, table), (x_at, x))
    copies = [pltpu.make_async_copy(a, b, arrived.at[i]) for i, (a, b) in enumerate(pairs)]
    for copy in copies:
        copy.start()
    half = table.shape[1] // 2
    at = lax.broadcasted_iota(jnp.int32, (8, half), 1).astype(F32)
    freq = jnp.exp(-math.log(10000.0) * at / half)
    line = lax.broadcasted_iota(jnp.int32, (8, half), 0)
    for copy in copies:
        copy.wait()
    slot = place[2]
    t_from, t_below = (plan[levels[place[2 + i]]].astype(F32) for i in range(2))
    angle = jnp.where(line < 3, t_from, t_below) * freq
    emb = jnp.concatenate([jnp.cos(angle), jnp.sin(angle)], axis=1)
    values = table[...]
    mods[...] = jnp.concatenate([values, values[:2], values], axis=0) + emb
    mods[5:6] = jnp.full((1, 2 * half), (jnp.where(slot > 0, t_below, 0.0) - t_from) / 1000.0, F32)
    mods[6:7] = jnp.full((1, 2 * half), jnp.where(slot == 0, 1.0, 0.0), F32)
    out[...] = norm_rows(x[...].astype(F32), mods[1:2], mods[0:1])


def start(place, levels, plan, x, table):
    vmem, smem = pl.BlockSpec(memory_space=pltpu.VMEM), pl.BlockSpec(memory_space=pltpu.SMEM)
    hbm = pl.BlockSpec(memory_space=pl.ANY)
    return pl.pallas_call(
        start_kernel,
        in_specs=[smem] + [hbm] * 4,
        out_specs=[vmem] * 2,
        out_shape=[jax.ShapeDtypeStruct(x.shape, BF16), jax.ShapeDtypeStruct((8, x.shape[1]), F32)],
        scratch_shapes=[
            pltpu.SMEM(levels.shape, jnp.int32),
            pltpu.SMEM(plan.shape, jnp.int32),
            pltpu.VMEM(x.shape, BF16),
            pltpu.VMEM(table.shape, F32),
            pltpu.SemaphoreType.DMA((4,)),
        ],
        compiler_params=pltpu.CompilerParams(vmem_limit_bytes=ALL_VMEM),
        name="start",
    )(place, levels, plan, x, table)


def stepped(x, mods, parts):
    mixed = parts[0][...].astype(F32)
    for part in parts[1:]:
        mixed += part[...].astype(F32)
    x = x[...].astype(F32)
    speed = (x + mods[2:3] * mixed).astype(BF16)
    return speed, (x + mods[5:6] * speed.astype(F32)).astype(BF16)


def middle_kernel(x, mods, fresh, *refs):
    parts, (speed_out, state_out, normed_out) = refs[:-3], refs[-3:]
    speed, new = stepped(x, mods, parts)
    speed_out[...] = speed
    state = jnp.where(mods[6:7] > 0.5, fresh[...].astype(F32), new.astype(F32))
    state_out[...] = state.astype(BF16)
    normed_out[...] = norm_rows(state, mods[4:5], mods[3:4])


def last_kernel(x, mods, before, *refs):
    parts, (speeds_out, new_out) = refs[:-2], refs[-2:]
    speed, new = stepped(x, mods, parts)
    speeds_out[0] = before[...]
    speeds_out[1] = speed
    new_out[...] = new


def update(kernel, name, x, mods, other, parts, shapes):
    vmem = pl.BlockSpec(memory_space=pltpu.VMEM)
    return pl.pallas_call(
        kernel,
        in_specs=[vmem] * (3 + len(parts)),
        out_specs=[vmem] * len(shapes),
        out_shape=[jax.ShapeDtypeStruct(shape, BF16) for shape in shapes],
        compiler_params=pltpu.CompilerParams(vmem_limit_bytes=VMEM_LIMIT),
        name=name,
    )(x, mods, other, *parts)


def one_down(array, dx, dy):
    queue = lax.axis_size("queue")
    pairs = [
        (q * 8 + y * 4 + x, ((q - 1) % queue) * 8 + ((y + dy) % 2) * 4 + (x + dx) % 4)
        for q in range(queue)
        for y in range(2)
        for x in range(4)
    ]
    return lax.ppermute(array, ("queue", "head"), pairs)


def gather_blocks(block, move):
    other = move(block, 0, 1)
    left, right, across = move(block, 1, 0), move(block, -1, 0), move(block, 2, 0)
    other_left, other_right = along_head(other, 1, 0), along_head(other, -1, 0)
    other_across = along_head(across, 0, 1)
    return [right, across, left, other, other_right, other_across, other_left]


def scatter_blocks(blocks):
    own, right, across, left, other, other_right, other_across, other_left = blocks
    add = lambda *terms: sum(term.astype(F32) for term in terms).astype(BF16)
    from_left, from_right = along_head(other_right, 1, 0), along_head(other_left, -1, 0)
    from_other = along_head(other_across, 0, 1)
    gets = [along_head(right, 1, 0), along_head(left, -1, 0)]
    gets.append(along_head(add(other, from_left, from_right), 0, 1))
    gets.append(along_head(add(across, from_other), 2, 0))
    return [own] + gets


def turned(sums, by):
    by *= HD // 4
    return jnp.concatenate([sums[:, by:], sums[:, :by]], axis=1)


def on_device(
    latent, fresh, levels, windows, plan, mod_table, w_query, w_key, w_value, w_out, query_gain, key_gain
):
    queue_count, head_count = lax.axis_size("queue"), lax.axis_size("head")
    slot = lax.axis_index("queue")
    rows = latent.shape[0]
    span = rows * head_count
    every = w_query.shape[1] * head_count
    side, z, core = slot // 8, (slot // 2) % 4, slot % 2
    place = jnp.stack([side, core, slot, (slot + queue_count - 1) % queue_count])
    places = jnp.stack(
        [
            ((side + s) % 2) * 8 + ((z + dz) % 4) * 2 + (core + c) % 2
            for dz in range(4)
            for s in range(2)
            for c in range(2)
        ]
    )
    lowers = jnp.maximum(0, jnp.arange(queue_count, dtype=jnp.int32) - windows + 1)
    order = jnp.concatenate([places[:4], lowers[places[:4]], places])

    gains = jnp.stack([key_gain, query_gain])

    x = latent
    normed, mods = start(place, levels, plan, x, mod_table)
    blocks = [normed] + gather_blocks(normed, along_head)
    weights = load([w_key, w_value, w_query])
    for step in range(STEPS):
        with jax.named_scope("project"):
            keep, send = project(place, blocks, *weights, gains)
        with jax.named_scope("swap"):
            swapped = along_queue(send, 0, 0, 1)
            near, far, queries, sums = assemble(keep, swapped)
        with jax.named_scope("round1"):
            near1, near3 = along_queue(near, 0, -1, 0), along_queue(near, 0, 1, 0)
            far = along_queue(far, 1, 0, 0)
            others = [along_head(sums, by, 0) for by in (1, 2, 3)]
            near1, near3, far, others = lax.optimization_barrier((near1, near3, far, others))
            for by in (1, 2, 3):
                sums += turned(others[by - 1], by)
        with jax.named_scope("round2"):
            other = along_head(sums, 0, 1)
            sums, near, far = append_sums(sums, other, near, far)
        with jax.named_scope("round3"):
            far1, far3 = along_queue(far, 0, -1, 0), along_queue(far, 0, 1, 0)
            near2 = along_queue(near, 0, -2, 0)
        with jax.named_scope("round4"):
            queries = collect_sums(queries, [near, far1, near2, far3])
            queries = along_queue(queries, 1, 0, 0)
            far2 = along_queue(far, 0, -2, 0)
        with jax.named_scope("attend"):
            if step > 0:
                state, queries = lax.optimization_barrier((state, queries))
                x = one_down(state, 0, 0)
            pairs = [near, near1, near2, near3, far, far1, far2, far3]
            o_far, keys, values, w_near = attend_far(order, pairs, queries, w_out, every)
            far = along_queue(o_far, 1, 0, 0)
            o_own, o_sib = attend_near(order, sums, keep, swapped, keys, values, every)
            far, o_sib = lax.optimization_barrier((far, o_sib))
            o_near = along_queue(o_sib, 0, 0, 1)
            near_far = along_queue(far, 0, 0, 1)
            if step > 0:
                near_far, x = lax.optimization_barrier((near_far, x))
        with jax.named_scope("mix"):
            product = mix(place, o_own, far, o_near, near_far, w_near)
        with jax.named_scope("scatter"):
            parts = scatter_blocks(product)
        shape = latent.shape
        if step < STEPS - 1:
            with jax.named_scope("update"):
                speed, state, normed = update(middle_kernel, "middle", x, mods, fresh, parts, [shape] * 3)
            with jax.named_scope("gather"):
                blocks = [one_down(normed, 0, 0)] + gather_blocks(normed, one_down)
                held = lax.optimization_barrier((w_key, w_value, w_query, normed))
                weights = load(held[:3])
        else:
            speeds, new = update(last_kernel, "last", x, mods, speed, parts, [(2, *shape), shape])
    return (speeds, new)


def solution(mesh):
    return jax.shard_map(
        on_device,
        mesh=mesh,
        in_specs=(
            P(("queue", "head"), None),
            P("head", None),
            P(),
            P(),
            P(),
            P(),
            P(None, "head"),
            P(None, "head"),
            P(None, "head"),
            P("head", None),
            P("head"),
            P("head"),
        ),
        out_specs=(P(None, ("queue", "head"), None), P(("queue", "head"), None)),
        check_vma=False,
    )
```
